128 devices in a mesh: tm: 16 (over x, z), chan: 8 (over y, core).
Axes of the slice: x: 4, y: 4, z: 4, core: 2. Of those that a mesh axis runs over, the one named last changes fastest.
Arguments:
- samples: float32 [8192, 65536], P('chan', 'tm'), as said below
- omega: float32 [4, 8192, 128], P(None, 'chan'), may hold values from -0.03125 to 0.03125
Outputs:
- basis: float32 [128, 65536], P(None, ('tm', 'chan'))
- projection: float32 [4, 8192, 128], P(None, 'chan')
The draws below stay inside these ranges and needn't reach their ends.
Inputs may be any that keep to these rules, and one draw needn't show every extreme that they name: The samples are real-valued (magnitude and angle channels of the phasor stream).
All inputs are finite; a program needn't handle non-finite values.
Results may differ from the reference program's by a relative error of at most 0.0001.
Values sent between devices are 32-bit elements; how exact they have to be, the bound alone decides.
No kernel may reach another device: no remote copies, remote signals or barrier semaphores. Data moves between devices by JAX's collectives and lax.ppermute only.
A program may use at most 128 MiB of HBM per device.

```python
import math
import jax
import jax.numpy as jnp
from jax import lax

C = 8192
R = 128
LAG = 512
LAGS = 4
TIME = 65536


def draw_samples(key, part):
    key = jax.random.fold_in(key, 7)
    first = jax.random.fold_in(key, 0)
    steps = jnp.arange(TIME, dtype=jnp.float32)
    envelope = jnp.exp(-1.2 * steps / TIME)[None, :]
    values = jax.random.normal(first, (C, TIME), jnp.float32)
    return values * envelope


def levels(stream_key, extent, shards, low, largest):
    def one(dim, blocks):
        steps = jax.random.uniform(jax.random.fold_in(jax.random.fold_in(stream_key, 6), dim), (blocks,), jnp.float32, low / len(shards), largest / len(shards))
        return jnp.repeat(jnp.exp(steps), extent[dim] // blocks).reshape((-1,) + (1,) * (len(extent) - dim - 1))

    factor_of = one(*shards[0])
    for cut in shards[1:]:
        factor_of = factor_of * one(*cut)
    return factor_of


def centred(own_key, shape, deviation, reach, shards=(), kind=jnp.bfloat16):
    result = deviation * jax.random.normal(own_key, shape, jnp.float32)
    if shards:
        result = result * levels(own_key, shape, shards, -0.22, 0.18)
    return jnp.clip(result, -reach, reach).astype(kind)


def setup_inputs(seed: int = 0) -> dict:
    streams_of = jax.random.split(jax.random.key(seed), 3)
    samples = draw_samples(jax.random.fold_in(streams_of[2], 71), 0)
    omega = centred(streams_of[1], (LAGS, C, R), (LAGS * C) ** -0.5, 0.03125, ((1, 8),), jnp.float32)
    return dict(samples=samples, omega=omega)


def reference(samples, omega):
    total = samples.shape[1]
    sketch = jnp.zeros((omega.shape[2], total), jnp.float32)
    for delay in range(LAGS):
        width = total - delay * LAG
        part = jnp.dot(omega[delay].T.astype(jnp.float32), samples[:, delay * LAG:].astype(jnp.float32), precision=lax.Precision.HIGHEST, preferred_element_type=jnp.float32)
        sketch = sketch.at[:, :width].add(part)
    gram = jnp.dot(sketch.astype(jnp.float32), sketch.T.astype(jnp.float32), precision=lax.Precision.HIGHEST, preferred_element_type=jnp.float32)
    lower = jnp.linalg.cholesky(gram)
    rows = lax.linalg.triangular_solve(lower, sketch, left_side=True, lower=True)
    blocks = []
    for delay in range(LAGS):
        width = total - delay * LAG
        blocks.append(jnp.dot(samples[:, delay * LAG:].astype(jnp.float32), rows[:, :width].T.astype(jnp.float32), precision=lax.Precision.HIGHEST, preferred_element_type=jnp.float32))
    projection = jnp.stack(blocks, 0)
    return (rows * math.sqrt(total), projection)
```

```python
import functools
import math

import jax
import jax.numpy as jnp
from jax import lax
from jax.experimental import pallas as pl
from jax.experimental.pallas import tpu as pltpu
from jax.sharding import Mesh
from jax.sharding import PartitionSpec as P

LAG = 512
F32 = jnp.float32
BF16 = jnp.bfloat16
NT = (((1,), (1,)), ((), ()))
NN = (((1,), (0,)), ((), ()))
MIB = 1024 * 1024


def split(value):
    high = value.astype(BF16)
    return high, (value - high.astype(F32)).astype(BF16)


def dot3(a_high, a_low, b_high, b_low, dims):
    dot = functools.partial(lax.dot_general, dimension_numbers=dims, preferred_element_type=F32)
    return dot(a_high, b_high) + (dot(a_high, b_low) + dot(a_low, b_high))


def whole(count):
    return [pl.BlockSpec(memory_space=pltpu.VMEM)] * count


def call(body, outs, args, limit=24):
    return pl.pallas_call(
        body,
        out_shape=[jax.ShapeDtypeStruct(shape, F32) for shape in outs],
        in_specs=whole(len(args)),
        out_specs=whole(len(outs)),
        compiler_params=pltpu.CompilerParams(vmem_limit_bytes=limit * MIB),
    )(*args)


def moved(value, axes, offset):
    count = lax.axis_size(axes)
    return lax.ppermute(value, axes, [(i, (i + offset) % count) for i in range(count)])


def shifted(value, axes, offset):
    count = lax.axis_size(axes)
    pairs = [(i, i + offset) for i in range(count) if 0 <= i + offset < count]
    return lax.ppermute(value, axes, pairs)


def sketch_partial(samples, omega):
    delays, channels, rank = omega.shape
    block = samples.shape[1]
    steps = block // LAG
    margin = (delays - 1) * LAG
    half = rank // 2

    def body(s_ref, o_ref, keep_ref, send_ref, high_ref, low_ref, acc_ref):
        step = pl.program_id(0)

        @pl.when(step == 0)
        def _():
            for d in range(delays):
                high, low = split(o_ref[d].T)
                high_ref[d * rank : (d + 1) * rank, :] = high
                low_ref[d * rank : (d + 1) * rank, :] = low
            acc_ref[...] = jnp.zeros_like(acc_ref)

        s_high, s_low = split(s_ref[...])
        term = dot3(high_ref[...], low_ref[...], s_high, s_low, NN)
        for d in range(delays):
            at = pl.ds(pl.multiple_of((step + delays - 1 - d) * LAG, LAG), LAG)
            acc_ref[:, at] += term[d * rank : (d + 1) * rank, :]

        @pl.when(step == steps - 1)
        def _():
            core = lax.axis_index("core")
            keep_ref[...] = acc_ref[pl.ds(pl.multiple_of(core * half, half), half), :]
            send_ref[...] = acc_ref[pl.ds(pl.multiple_of((1 - core) * half, half), half), :]

    out = jax.ShapeDtypeStruct((half, margin + block), F32)
    spec = pl.BlockSpec((half, margin + block), lambda i: (0, 0))
    return pl.pallas_call(
        body,
        grid=(steps,),
        out_shape=[out, out],
        in_specs=[
            pl.BlockSpec((channels, LAG), lambda i: (0, i)),
            pl.BlockSpec(omega.shape, lambda i: (0, 0, 0)),
        ],
        out_specs=[spec, spec],
        scratch_shapes=[
            pltpu.VMEM((delays * rank, channels), BF16),
            pltpu.VMEM((delays * rank, channels), BF16),
            pltpu.VMEM((rank, margin + block), F32),
        ],
        compiler_params=pltpu.CompilerParams(vmem_limit_bytes=40 * MIB),
        cost_estimate=pl.CostEstimate(
            flops=6 * delays * rank * channels * block, bytes_accessed=samples.size * 4, transcendentals=0
        ),
    )(samples, omega)


def projection_partial(samples, mine, other, delays):
    channels, block = samples.shape
    half, width = mine.shape
    rank = 2 * half
    steps = block // LAG
    piece = channels // 8
    lanes = delays * rank
    gram_rows = rank // delays

    def body(s_ref, mine_ref, other_ref, *refs):
        outs = refs[:8]
        high_ref, low_ref, acc_ref, gram_ref = refs[8:]
        step = pl.program_id(0)

        @pl.when(step == 0)
        def _():
            core = lax.axis_index("core")
            for ref, place in ((mine_ref, core), (other_ref, 1 - core)):
                high, low = split(ref[...])
                at = pl.ds(pl.multiple_of(place * half, half), half)
                high_ref[at, :] = high
                low_ref[at, :] = low
            acc_ref[...] = jnp.zeros_like(acc_ref)
            gram_ref[...] = jnp.zeros_like(gram_ref)

        s_high, s_low = split(s_ref[...])
        highs, lows = [], []
        for d in range(delays):
            at = pl.ds(pl.multiple_of((step + delays - 1 - d) * LAG, LAG), LAG)
            highs.append(high_ref[:, at])
            lows.append(low_ref[:, at])
        gram_ref[...] += dot3(highs[0], lows[0], highs[0], lows[0], NT)
        acc_ref[...] += dot3(s_high, s_low, jnp.concatenate(highs, 0), jnp.concatenate(lows, 0), NT)

        @pl.when(step == steps - 1)
        def _():
            for route, axis in enumerate(("x", "z")):
                here = lax.axis_index(axis)
                for k in range(4):
                    row = route * 4 * piece + lax.rem(here + k, 4) * piece
                    outs[route * 4 + k][:piece, :] = acc_ref[pl.ds(pl.multiple_of(row, piece), piece), :]
            for k in range(4):
                for d in range(delays):
                    outs[k][piece:, d * rank : (d + 1) * rank] = gram_ref[d * gram_rows : (d + 1) * gram_rows, :]

    shapes = [(piece + gram_rows, lanes)] * 4 + [(piece, lanes)] * 4
    return pl.pallas_call(
        body,
        grid=(steps,),
        out_shape=[jax.ShapeDtypeStruct(s, F32) for s in shapes],
        in_specs=[
            pl.BlockSpec((channels, LAG), lambda i: (0, i)),
            pl.BlockSpec((half, width), lambda i: (0, 0)),
            pl.BlockSpec((half, width), lambda i: (0, 0)),
        ],
        out_specs=[pl.BlockSpec(s, lambda i: (0, 0)) for s in shapes],
        scratch_shapes=[
            pltpu.VMEM((rank, width), BF16),
            pltpu.VMEM((rank, width), BF16),
            pltpu.VMEM((channels, lanes), F32),
            pltpu.VMEM((rank, rank), F32),
        ],
        compiler_params=pltpu.CompilerParams(vmem_limit_bytes=40 * MIB),
        cost_estimate=pl.CostEstimate(
            flops=6 * lanes * channels * block, bytes_accessed=samples.size * 4, transcendentals=0
        ),
    )(samples, mine, other)


def shards(samples, omega):
    delays, channels, rank = omega.shape
    block = samples.shape[1]
    margin = (delays - 1) * LAG
    width = margin + block
    half, share = rank // 2, rank // 8
    total = block * lax.axis_size(("x", "z"))

    keep, send = sketch_partial(samples, omega)
    came = moved(send, "core", 1)

    def add_cores(a_ref, b_ref, *outs):
        y = lax.axis_index("y")
        for k in range(4):
            at = pl.ds(pl.multiple_of(lax.rem(y + k, 4) * share, share), share)
            outs[k][...] = a_ref[at, :] + b_ref[at, :]

    parts = call(add_cores, [(share, width)] * 4, [keep, came])
    parts = [parts[0]] + [moved(parts[k], "y", k) for k in (1, 2, 3)]

    def add_chips(a_ref, b_ref, c_ref, d_ref, main_ref, rim_ref):
        value = (a_ref[...] + b_ref[...]) + (c_ref[...] + d_ref[...])
        main_ref[...] = value[:, margin:]
        rim_ref[...] = value[:, :margin]

    main, rim = call(add_chips, [(share, block), (share, margin)], parts)
    rim = shifted(rim, ("x", "z"), -1)

    def add_rim(main_ref, rim_ref, out_ref, last_ref):
        out_ref[...] = main_ref[...]
        value = main_ref[:, block - margin :] + rim_ref[...]
        out_ref[:, block - margin :] = value
        last_ref[...] = value

    main, last = call(add_rim, [(share, block), (share, margin)], [main, rim])
    before = shifted(last, ("x", "z"), 1)

    def join(before_ref, main_ref, out_ref):
        out_ref[:, :margin] = before_ref[...]
        out_ref[:, margin:] = main_ref[...]

    (own,) = call(join, [(share, width)], [before, main])
    rows = [own] + [moved(own, "y", k) for k in (1, 2, 3)]

    def order(a_ref, b_ref, c_ref, d_ref, out_ref):
        y = lax.axis_index("y")
        for k, ref in enumerate((a_ref, b_ref, c_ref, d_ref)):
            at = pl.ds(pl.multiple_of(lax.rem(y - k + 4, 4) * share, share), share)
            out_ref[at, :] = ref[...]

    (mine,) = call(order, [(half, width)], rows)
    other = moved(mine, "core", 1)

    pieces = projection_partial(samples, mine, other, delays)
    first = [pieces[0]] + [moved(pieces[k], "x", k) for k in (1, 2, 3)]
    second = [pieces[4]] + [moved(pieces[4 + k], "z", k) for k in (1, 2, 3)]
    piece, lanes = channels // 8, delays * rank
    quarter = piece // 4
    gram_rows = rank // delays

    def add_first(*refs):
        ins, outs = refs[:8], refs[8:]
        value = (ins[0][...] + ins[1][...]) + (ins[2][...] + ins[3][...])
        outs[0][...] = value
        value = (ins[4][...] + ins[5][...]) + (ins[6][...] + ins[7][...])
        outs[1][...] = value
        z, x = lax.axis_index("z"), lax.axis_index("x")
        for k in range(4):
            at = pl.ds(pl.multiple_of(lax.rem(z + k, 4) * quarter, quarter), quarter)
            outs[2 + k][:quarter, :] = outs[0][at, :]
            outs[2 + k][quarter:, :] = outs[0][piece:, :]
            at = pl.ds(pl.multiple_of(lax.rem(x + k, 4) * quarter, quarter), quarter)
            outs[6 + k][...] = outs[1][at, :]

    sums = call(
        add_first,
        [(piece + gram_rows, lanes), (piece, lanes)]
        + [(quarter + gram_rows, lanes)] * 4
        + [(quarter, lanes)] * 4,
        first + second,
    )[2:]
    first = [sums[0]] + [moved(sums[k], "z", k) for k in (1, 2, 3)]
    second = [sums[4]] + [moved(sums[4 + k], "x", k) for k in (1, 2, 3)]

    def add_second(*refs):
        ins, (one_ref, two_ref, gram_ref) = refs[:8], refs[8:]
        value = (ins[0][...] + ins[1][...]) + (ins[2][...] + ins[3][...])
        one_ref[...] = value[:quarter, :]
        for d in range(delays):
            gram_ref[d * gram_rows : (d + 1) * gram_rows, :] = value[quarter:, d * rank : (d + 1) * rank]
        two_ref[...] = (ins[4][...] + ins[5][...]) + (ins[6][...] + ins[7][...])

    one, two, gram = call(
        add_second, [(quarter, lanes), (quarter, lanes), (rank, rank)], first + second
    )
    first = [one] + [moved(one, "z", k) for k in (1, 2, 3)]
    second = [two] + [moved(two, "x", k) for k in (1, 2, 3)]

    def arrange(*refs):
        ins, outs = refs[:8], refs[8:]
        for route, axis in enumerate(("z", "x")):
            here = lax.axis_index(axis)
            for k in range(4):
                at = pl.ds(pl.multiple_of(lax.rem(here - k + 4, 4) * quarter, quarter), quarter)
                outs[route][at, :] = ins[route * 4 + k][...]

    one, two = call(arrange, [(piece, lanes)] * 2, first + second)
    first = [one] + [moved(one, "x", k) for k in (1, 2, 3)]
    second = [two] + [moved(two, "z", k) for k in (1, 2, 3)]

    lower = jnp.linalg.cholesky(gram)
    inverse = lax.linalg.triangular_solve(lower, jnp.eye(rank, dtype=F32), left_side=True, lower=True)

    def finish(*refs):
        inverse_ref, mine_ref, other_ref = refs[:3]
        ins, (basis_ref, out_ref) = refs[3:11], refs[11:]
        high, low = split(inverse_ref[...])
        for route, axis in enumerate(("x", "z")):
            here = lax.axis_index(axis)
            for k in range(4):
                row = route * 4 * piece + lax.rem(here - k + 4, 4) * piece
                at = pl.ds(pl.multiple_of(row, piece), piece)
                for d in range(delays):
                    a_high, a_low = split(ins[route * 4 + k][:, d * rank : (d + 1) * rank])
                    out_ref[d, at, :] = dot3(a_high, a_low, high, low, NT)
        core, y = lax.axis_index("core"), lax.axis_index("y")
        columns = block // 8
        at = pl.ds(pl.multiple_of(margin + (y * 2 + core) * columns, columns), columns)
        sketch = jnp.concatenate([mine_ref[:, at], other_ref[:, at]], 0)
        swapped = jnp.concatenate([other_ref[:, at], mine_ref[:, at]], 0)
        sketch = jnp.where(core == 0, sketch, swapped)
        s_high, s_low = split(sketch)
        basis_ref[...] = math.sqrt(total) * dot3(high, low, s_high, s_low, NN)

    basis, projection = call(
        finish,
        [(rank, block // 8), (delays, channels, rank)],
        [inverse, mine, other] + first + second,
        40,
    )
    return basis, projection


def solution(mesh):
    fine = Mesh(mesh.devices.reshape(4, 4, 4, 2), ("x", "z", "y", "core"))
    tm, chan = ("x", "z"), ("y", "core")
    return jax.shard_map(
        shards,
        mesh=fine,
        in_specs=(P(chan, tm), P(None, chan, None)),
        out_specs=(P(None, tm + chan), P(None, chan, None)),
        check_vma=False,
    )
```

```python
import functools
import math

import jax
import jax.numpy as jnp
from jax import lax
from jax.experimental import pallas as pl
from jax.experimental.pallas import tpu as pltpu
from jax.sharding import Mesh
from jax.sharding import PartitionSpec as P

LAG = 512
WIDE = 1024
F32 = jnp.float32
BF16 = jnp.bfloat16
NT = (((1,), (1,)), ((), ()))
NN = (((1,), (0,)), ((), ()))
MIB = 1024 * 1024


def split(value):
    high = value.astype(BF16)
    return high, (value - high.astype(F32)).astype(BF16)


def dot3(a_high, a_low, b_high, b_low, dims):
    dot = functools.partial(lax.dot_general, dimension_numbers=dims, preferred_element_type=F32)
    return dot(a_high, b_high) + (dot(a_high, b_low) + dot(a_low, b_high))


def whole(count):
    return [pl.BlockSpec(memory_space=pltpu.VMEM)] * count


def call(body, outs, args, limit=24):
    return pl.pallas_call(
        body,
        out_shape=[jax.ShapeDtypeStruct(shape, F32) for shape in outs],
        in_specs=whole(len(args)),
        out_specs=whole(len(outs)),
        compiler_params=pltpu.CompilerParams(vmem_limit_bytes=limit * MIB),
    )(*args)


AXES = ("x", "z", "y", "core")
SIDE = 4


def along(axis, step, value, blocks=0):
    pairs = []
    for x in range(SIDE):
        for z in range(SIDE):
            for y in range(SIDE):
                for core in range(2):
                    flip = 0 if step is None else (1, 3)[step ^ core]
                    there = {"x": x, "z": z, "y": y}
                    there[axis] ^= flip
                    time = there["x"] * SIDE + there["z"] + blocks
                    if 0 <= time < SIDE * SIDE:
                        pairs.append((index(x, z, y, core), index(time // SIDE, time % SIDE, there["y"], core)))
    return lax.ppermute(value, AXES, pairs)


def index(x, z, y, core):
    return ((x * SIDE + z) * SIDE + y) * 2 + core


def side(axis, step):
    place = lax.axis_index(axis)
    upper = place // 2
    even = lax.rem(place + upper, 2)
    core = lax.axis_index("core")
    return even + (upper - even) * core if step == 0 else upper + (even - upper) * core


def rows_at(which, count):
    return pl.ds(pl.multiple_of(which * count, count), count)


def sketch_partial(samples, omega):
    delays, channels, rank = omega.shape
    block = samples.shape[1]
    steps = block // LAG
    margin = (delays - 1) * LAG
    half = rank // 2

    def body(s_ref, o_ref, keep_ref, send_ref, high_ref, low_ref, acc_ref):
        step = pl.program_id(0)

        @pl.when(step == 0)
        def _():
            for d in range(delays):
                high, low = split(o_ref[d].T)
                high_ref[d * rank : (d + 1) * rank, :] = high
                low_ref[d * rank : (d + 1) * rank, :] = low
            acc_ref[...] = jnp.zeros_like(acc_ref)

        s_high, s_low = split(s_ref[...])
        term = dot3(high_ref[...], low_ref[...], s_high, s_low, NN)
        for d in range(delays):
            at = pl.ds(pl.multiple_of((step + delays - 1 - d) * LAG, LAG), LAG)
            acc_ref[:, at] += term[d * rank : (d + 1) * rank, :]

        @pl.when(step == steps - 1)
        def _():
            core = lax.axis_index("core")
            keep_ref[...] = acc_ref[pl.ds(pl.multiple_of(core * half, half), half), :]
            send_ref[...] = acc_ref[pl.ds(pl.multiple_of((1 - core) * half, half), half), :]

    out = jax.ShapeDtypeStruct((half, margin + block), F32)
    spec = pl.BlockSpec((half, margin + block), lambda i: (0, 0))
    return pl.pallas_call(
        body,
        grid=(steps,),
        out_shape=[out, out],
        in_specs=[
            pl.BlockSpec((channels, LAG), lambda i: (0, i)),
            pl.BlockSpec(omega.shape, lambda i: (0, 0, 0)),
        ],
        out_specs=[spec, spec],
        scratch_shapes=[
            pltpu.VMEM((delays * rank, channels), BF16),
            pltpu.VMEM((delays * rank, channels), BF16),
            pltpu.VMEM((rank, margin + block), F32),
        ],
        compiler_params=pltpu.CompilerParams(vmem_limit_bytes=40 * MIB),
        cost_estimate=pl.CostEstimate(
            flops=6 * delays * rank * channels * block, bytes_accessed=samples.size * 4, transcendentals=0
        ),
    )(samples, omega)


def projection_partial(samples, mine, other, delays, part, axis):
    channels, block = samples.shape
    half, width = mine.shape
    rank = 2 * half
    steps = block // WIDE
    rows = channels // 2
    lanes = delays * rank
    tail = rank // delays if part == 0 else 0

    def body(s_ref, mine_ref, other_ref, keep_ref, send_ref, high_ref, low_ref, acc_ref, gram_ref):
        step = pl.program_id(0)

        @pl.when(step == 0)
        def _():
            core = lax.axis_index("core")
            for ref, place in ((mine_ref, core), (other_ref, 1 - core)):
                high, low = split(ref[...])
                high_ref[rows_at(place, half), :] = high
                low_ref[rows_at(place, half), :] = low
            acc_ref[...] = jnp.zeros_like(acc_ref)
            gram_ref[...] = jnp.zeros_like(gram_ref)

        s_high, s_low = split(s_ref[...])
        highs, lows = [], []
        for d in range(delays):
            at = pl.ds(pl.multiple_of(step * WIDE + (delays - 1 - d) * LAG, LAG), WIDE)
            highs.append(high_ref[:, at])
            lows.append(low_ref[:, at])
        if part == 0:
            gram_ref[...] += dot3(highs[0], lows[0], highs[0], lows[0], NT)
        acc_ref[...] += dot3(s_high, s_low, jnp.concatenate(highs, 0), jnp.concatenate(lows, 0), NT)

        @pl.when(step == steps - 1)
        def _():
            which = side(axis, 0)
            for place, ref in ((which, keep_ref), (1 - which, send_ref)):
                ref[: rows // 2, :] = acc_ref[rows_at(place, rows // 2), :]
                for d in range(delays if tail else 0):
                    ref[rows // 2 :, d * rank : (d + 1) * rank] = gram_ref[d * tail : (d + 1) * tail, :]

    shape = (rows // 2 + tail, lanes)
    return pl.pallas_call(
        body,
        grid=(steps,),
        out_shape=[jax.ShapeDtypeStruct(shape, F32)] * 2,
        in_specs=[
            pl.BlockSpec((rows, WIDE), lambda i: (part, i)),
            pl.BlockSpec((half, width), lambda i: (0, 0)),
            pl.BlockSpec((half, width), lambda i: (0, 0)),
        ],
        out_specs=[pl.BlockSpec(shape, lambda i: (0, 0))] * 2,
        scratch_shapes=[
            pltpu.VMEM((rank, width), BF16),
            pltpu.VMEM((rank, width), BF16),
            pltpu.VMEM((rows, lanes), F32),
            pltpu.VMEM((rank, rank), F32),
        ],
        compiler_params=pltpu.CompilerParams(vmem_limit_bytes=36 * MIB),
        cost_estimate=pl.CostEstimate(
            flops=6 * lanes * rows * block, bytes_accessed=rows * block * 4, transcendentals=0
        ),
    )(samples, mine, other)


def fold(keep, came, axis, step, tail=0):
    count = (keep.shape[0] - tail) // 2

    def body(a_ref, b_ref, keep_ref, send_ref):
        which = side(axis, step)
        for place, ref in ((which, keep_ref), (1 - which, send_ref)):
            at = rows_at(place, count)
            ref[:count, :] = a_ref[at, :] + b_ref[at, :]
            if tail:
                ref[count:, :] = a_ref[2 * count :, :] + b_ref[2 * count :, :]

    return call(body, [(count + tail, keep.shape[1])] * 2, [keep, came], 8)


def add(a, b, tail=0):
    count = a.shape[0] - tail

    def body(a_ref, b_ref, out_ref, *tails):
        out_ref[...] = a_ref[:count, :] + b_ref[:count, :]
        for ref in tails:
            ref[...] = a_ref[count:, :] + b_ref[count:, :]

    return call(body, [(count, a.shape[1])] + [(tail, a.shape[1])] * (tail > 0), [a, b], 8)


def unfold(mine, came, axis, step):
    count = mine.shape[0]

    def body(a_ref, b_ref, out_ref):
        out_ref[rows_at(side(axis, step), count), :] = a_ref[...]
        out_ref[rows_at(1 - side(axis, step), count), :] = b_ref[...]

    return call(body, [(2 * count, mine.shape[1])], [mine, came], 8)[0]


def summed(keep, send, one, two, tail=0):
    keep, send = fold(keep, along(one, 0, send), one, 1, tail)
    (value,) = add(keep, along(one, 1, send))
    (value,) = add(value, along(two, 0, value))
    value, *rest = add(value, along(two, 1, value), tail)
    value = unfold(value, along(one, 1, value), one, 1)
    return (value, along(one, 0, value), *rest)


def inverse_factor(tail, rank):
    deep, delays = tail.shape[0], tail.shape[1] // rank
    panel = 16

    def body(tail_ref, out_ref, left_ref, right_ref):
        for d in range(delays):
            left_ref[d * deep : (d + 1) * deep, :] = tail_ref[:, d * rank : (d + 1) * rank]
        square = (rank, rank)
        same = lax.broadcasted_iota(jnp.int32, square, 0) == lax.broadcasted_iota(jnp.int32, square, 1)
        right_ref[...] = jnp.where(same, 1.0, 0.0)
        row = lax.broadcasted_iota(jnp.int32, (panel, rank), 0)
        for top in range(0, rank, panel):
            end = top + panel
            left, right = left_ref[top:end, :], right_ref[top:end, :]
            columns = [jnp.broadcast_to(left[:, top + m : top + m + 1], (panel, rank)) for m in range(panel)]
            pivots = jnp.zeros((panel, rank), F32)
            for j in range(panel):
                reciprocal = 1.0 / columns[j][j : j + 1, :]
                pivots = jnp.where(row == j, reciprocal, pivots)
                factor = jnp.where(row > j, columns[j] * reciprocal, 0.0)
                for m in range(j + 1, panel):
                    columns[m] = columns[m] - factor * columns[m][j : j + 1, :]
                left = left - factor * left[j : j + 1, :]
                right = right - factor * right[j : j + 1, :]
            if end < rank:
                factors = (left * pivots).T
                below_left, below_right = left_ref[end:, :], right_ref[end:, :]
                for j in range(panel):
                    factor = factors[end:, j : j + 1]
                    below_left = below_left - factor * left[j : j + 1, :]
                    below_right = below_right - factor * right[j : j + 1, :]
                left_ref[end:, :] = below_left
                right_ref[end:, :] = below_right
            out_ref[top:end, :] = right * lax.sqrt(pivots)

    return pl.pallas_call(
        body,
        out_shape=jax.ShapeDtypeStruct((rank, rank), F32),
        in_specs=whole(1),
        out_specs=whole(1)[0],
        scratch_shapes=[pltpu.VMEM((rank, rank), F32)] * 2,
        compiler_params=pltpu.CompilerParams(vmem_limit_bytes=8 * MIB),
    )(tail)


def shards(samples, omega):
    delays, channels, rank = omega.shape
    block = samples.shape[1]
    margin = (delays - 1) * LAG
    width = margin + block
    half, share = rank // 2, rank // 4
    total = block * SIDE * SIDE

    keep, send = sketch_partial(samples, omega)
    came = lax.ppermute(send, "core", [(0, 1), (1, 0)])
    keep, send = fold(keep, came, "y", 0)
    came = along("y", 0, send)

    def add_chips(a_ref, b_ref, main_ref, rim_ref):
        main_ref[...] = a_ref[:, margin:] + b_ref[:, margin:]
        rim_ref[...] = a_ref[:, :margin] + b_ref[:, :margin]

    main, rim = call(add_chips, [(share, block), (share, margin)], [keep, came], 8)
    rim_one = along("y", None, rim, -1)
    rim_two = along("y", 1, rim, -1)
    came = along("y", 1, main)

    def add_rim(main_ref, came_ref, one_ref, two_ref, out_ref, last_ref):
        inner = block - margin
        out_ref[:, :inner] = main_ref[:, :inner] + came_ref[:, :inner]
        value = (main_ref[:, inner:] + came_ref[:, inner:]) + (one_ref[...] + two_ref[...])
        out_ref[:, inner:] = value
        last_ref[...] = value

    main, last = call(add_rim, [(share, block), (share, margin)], [main, came, rim_one, rim_two], 8)

    before = along("y", None, last, 1)
    before_came = along("y", 0, last, 1)
    came = along("y", 0, main)

    def join(before_ref, main_ref, before_came_ref, came_ref, out_ref):
        which = side("y", 0)
        for place, rim_ref, ref in ((which, before_ref, main_ref), (1 - which, before_came_ref, came_ref)):
            out_ref[rows_at(place, share), :margin] = rim_ref[...]
            out_ref[rows_at(place, share), margin:] = ref[...]

    (mine,) = call(join, [(half, width)], [before, main, before_came, came], 8)
    other = lax.ppermute(mine, "core", [(0, 1), (1, 0)])

    first = projection_partial(samples, mine, other, delays, 0, "x")
    second = projection_partial(samples, mine, other, delays, 1, "z")
    first, first_came, gram = summed(*first, "x", "z", rank // delays)
    second, second_came = summed(*second, "z", "x")
    inverse = inverse_factor(gram, rank)

    def finish(inverse_ref, mine_ref, other_ref, *refs):
        ins, (basis_ref, out_ref) = refs[:4], refs[4:]
        high, low = split(inverse_ref[...])
        count = channels // 4
        for part, axis in enumerate(("x", "z")):
            which = side(axis, 0)
            for place, ref in ((which, ins[2 * part]), (1 - which, ins[2 * part + 1])):
                at = pl.ds(pl.multiple_of((2 * part + place) * count, count), count)
                for d in range(delays):
                    a_high, a_low = split(ref[:, d * rank : (d + 1) * rank])
                    out_ref[d, at, :] = dot3(a_high, a_low, high, low, NT)
        core, y = lax.axis_index("core"), lax.axis_index("y")
        columns = block // 8
        at = pl.ds(pl.multiple_of(margin + (y * 2 + core) * columns, columns), columns)
        sketch = jnp.concatenate([mine_ref[:, at], other_ref[:, at]], 0)
        swapped = jnp.concatenate([other_ref[:, at], mine_ref[:, at]], 0)
        s_high, s_low = split(jnp.where(core == 0, sketch, swapped))
        basis_ref[...] = math.sqrt(total) * dot3(high, low, s_high, s_low, NN)

    basis, projection = call(
        finish,
        [(rank, block // 8), (delays, channels, rank)],
        [inverse, mine, other, first, first_came, second, second_came],
        24,
    )
    return basis, projection


def solution(mesh):
    fine = Mesh(mesh.devices.reshape(SIDE, SIDE, SIDE, 2), AXES)
    tm, chan = ("x", "z"), ("y", "core")
    return jax.shard_map(
        shards,
        mesh=fine,
        in_specs=(P(chan, tm), P(None, chan, None)),
        out_specs=(P(None, tm + chan), P(None, chan, None)),
        check_vma=False,
    )
```

```python
import functools
import math

import jax
import jax.numpy as jnp
from jax import lax
from jax.experimental import pallas as pl
from jax.experimental.pallas import tpu as pltpu
from jax.sharding import Mesh
from jax.sharding import PartitionSpec as P

LAG = 512
WIDE = 1024
F32 = jnp.float32
BF16 = jnp.bfloat16
NT = (((1,), (1,)), ((), ()))
NN = (((1,), (0,)), ((), ()))
MIB = 1024 * 1024


def split(value):
    high = value.astype(BF16)
    return high, (value - high.astype(F32)).astype(BF16)


def dot3(a_high, a_low, b_high, b_low, dims):
    dot = functools.partial(lax.dot_general, dimension_numbers=dims, preferred_element_type=F32)
    return dot(a_high, b_high) + (dot(a_high, b_low) + dot(a_low, b_high))


def whole(count):
    return [pl.BlockSpec(memory_space=pltpu.VMEM)] * count


def call(body, outs, args, limit=24, scratch=()):
    return pl.pallas_call(
        body,
        out_shape=[jax.ShapeDtypeStruct(shape, F32) for shape in outs],
        in_specs=whole(len(args)),
        out_specs=whole(len(outs)),
        scratch_shapes=[pltpu.VMEM(shape, F32) for shape in scratch],
        compiler_params=pltpu.CompilerParams(vmem_limit_bytes=limit * MIB),
    )(*args)


AXES = ("x", "z", "y", "core")
SIDE = 4


def along(axis, step, value, blocks=0):
    pairs = []
    for x in range(SIDE):
        for z in range(SIDE):
            for y in range(SIDE):
                for core in range(2):
                    flip = 0 if step is None else (1, 3)[step ^ core]
                    there = {"x": x, "z": z, "y": y}
                    there[axis] ^= flip
                    time = there["x"] * SIDE + there["z"] + blocks
                    if 0 <= time < SIDE * SIDE:
                        pairs.append((index(x, z, y, core), index(time // SIDE, time % SIDE, there["y"], core)))
    return lax.ppermute(value, AXES, pairs)


def index(x, z, y, core):
    return ((x * SIDE + z) * SIDE + y) * 2 + core


def side(axis, step, core=None):
    place = lax.axis_index(axis)
    upper = place // 2
    even = lax.rem(place + upper, 2)
    core = lax.axis_index("core") if core is None else core
    return even + (upper - even) * core if step == 0 else upper + (even - upper) * core


def rows_at(which, count):
    return pl.ds(pl.multiple_of(which * count, count), count)


def sketch_partial(samples, omega):
    delays, channels, rank = omega.shape
    block = samples.shape[1]
    steps = block // LAG
    margin = (delays - 1) * LAG
    half = rank // 2

    def body(s_ref, o_ref, keep_ref, send_ref, high_ref, low_ref, acc_ref):
        step = pl.program_id(0)

        @pl.when(step == 0)
        def _():
            for d in range(delays):
                high, low = split(o_ref[d].T)
                high_ref[d * rank : (d + 1) * rank, :] = high
                low_ref[d * rank : (d + 1) * rank, :] = low
            acc_ref[...] = jnp.zeros_like(acc_ref)

        s_high, s_low = split(s_ref[...])
        term = dot3(high_ref[...], low_ref[...], s_high, s_low, NN)
        for d in range(delays):
            at = pl.ds(pl.multiple_of((step + delays - 1 - d) * LAG, LAG), LAG)
            acc_ref[:, at] += term[d * rank : (d + 1) * rank, :]

        @pl.when(step == steps - 1)
        def _():
            core = lax.axis_index("core")
            keep_ref[...] = acc_ref[rows_at(core, half), :]
            send_ref[...] = acc_ref[rows_at(1 - core, half), :]

    out = jax.ShapeDtypeStruct((half, margin + block), F32)
    spec = pl.BlockSpec((half, margin + block), lambda i: (0, 0))
    return pl.pallas_call(
        body,
        grid=(steps,),
        out_shape=[out, out],
        in_specs=[
            pl.BlockSpec((channels, LAG), lambda i: (0, i)),
            pl.BlockSpec(omega.shape, lambda i: (0, 0, 0)),
        ],
        out_specs=[spec, spec],
        scratch_shapes=[
            pltpu.VMEM((delays * rank, channels), BF16),
            pltpu.VMEM((delays * rank, channels), BF16),
            pltpu.VMEM((rank, margin + block), F32),
        ],
        compiler_params=pltpu.CompilerParams(vmem_limit_bytes=40 * MIB),
        cost_estimate=pl.CostEstimate(
            flops=6 * delays * rank * channels * block, bytes_accessed=samples.size * 4, transcendentals=0
        ),
    )(samples, pltpu.with_memory_space_constraint(omega, pltpu.HBM))


def quarters():
    core = lax.axis_index("core")
    own, other = side("y", 0), side("y", 0, 1 - core)
    return [2 * core + own, 2 * (1 - core) + other, 2 * core + 1 - own, 2 * (1 - core) + 1 - other]


def in_order(places):
    return jnp.minimum(*places), jnp.maximum(*places)


def projection_partial(samples, sketches, delays, axis, gram):
    channels, block = samples.shape
    quarter, width = sketches[0][0].shape
    count = 2 * quarter
    rank = 2 * count
    steps = block // WIDE
    lanes = delays * count
    tail = rank * rank // lanes if gram else 0
    flat = [half for pair in sketches for half in pair]

    def body(s_ref, *refs):
        ins, (keep_ref, send_ref, high_ref, low_ref, acc_ref, gram_ref) = refs[: len(flat)], refs[len(flat) :]
        step = pl.program_id(0)

        @pl.when(step == 0)
        def _():
            for place, ref in zip(quarters(), ins):
                high, low = split(ref[...])
                high_ref[rows_at(place, quarter), :] = high
                low_ref[rows_at(place, quarter), :] = low
            acc_ref[...] = jnp.zeros_like(acc_ref)
            gram_ref[...] = jnp.zeros_like(gram_ref)

        s_high, s_low = split(s_ref[...])
        highs, lows = [], []
        for d in range(delays):
            at = pl.ds(pl.multiple_of(step * WIDE + (delays - 1 - d) * LAG, LAG), WIDE)
            for place in in_order(quarters()[len(flat) - 2 : len(flat)]):
                highs.append(high_ref[rows_at(place, quarter), at])
                lows.append(low_ref[rows_at(place, quarter), at])
        if gram:
            at = pl.ds(pl.multiple_of(step * WIDE + (delays - 1) * LAG, LAG), WIDE)
            high, low = high_ref[:, at], low_ref[:, at]
            gram_ref[...] += dot3(high, low, high, low, NT)
        acc_ref[...] += dot3(s_high, s_low, jnp.concatenate(highs, 0), jnp.concatenate(lows, 0), NT)

        @pl.when(step == steps - 1)
        def _():
            which = side(axis, 0)
            for place, ref in ((which, keep_ref), (1 - which, send_ref)):
                ref[: channels // 2, :] = acc_ref[rows_at(place, channels // 2), :]
                for group in range(lanes // rank if gram else 0):
                    ref[channels // 2 :, group * rank : (group + 1) * rank] = gram_ref[group * tail : (group + 1) * tail, :]

    shape = (channels // 2 + tail, lanes)
    return pl.pallas_call(
        body,
        grid=(steps,),
        out_shape=[jax.ShapeDtypeStruct(shape, F32)] * 2,
        in_specs=[pl.BlockSpec((channels, WIDE), lambda i: (0, i))]
        + [pl.BlockSpec((quarter, width), lambda i: (0, 0))] * len(flat),
        out_specs=[pl.BlockSpec(shape, lambda i: (0, 0))] * 2,
        scratch_shapes=[
            pltpu.VMEM((rank, width), BF16),
            pltpu.VMEM((rank, width), BF16),
            pltpu.VMEM((channels, lanes), F32),
            pltpu.VMEM((rank, rank), F32),
        ],
        compiler_params=pltpu.CompilerParams(vmem_limit_bytes=36 * MIB),
        cost_estimate=pl.CostEstimate(
            flops=6 * lanes * channels * block, bytes_accessed=channels * block * 4, transcendentals=0
        ),
    )(samples, *flat)


def fold(keep, came, axis, step, tail=0):
    count = (keep.shape[0] - tail) // 2

    def body(a_ref, b_ref, keep_ref, send_ref):
        which = side(axis, step)
        for place, ref in ((which, keep_ref), (1 - which, send_ref)):
            at = rows_at(place, count)
            ref[:count, :] = a_ref[at, :] + b_ref[at, :]
            if tail:
                ref[count:, :] = a_ref[2 * count :, :] + b_ref[2 * count :, :]

    return call(body, [(count + tail, keep.shape[1])] * 2, [keep, came], 8)


def add(a, b, tail=0):
    count = a.shape[0] - tail

    def body(a_ref, b_ref, out_ref, *tails):
        out_ref[...] = a_ref[:count, :] + b_ref[:count, :]
        for ref in tails:
            ref[...] = a_ref[count:, :] + b_ref[count:, :]

    return call(body, [(count, a.shape[1])] + [(tail, a.shape[1])] * (tail > 0), [a, b], 8)


def unfold(mine, came, axis, step):
    count = mine.shape[0]

    def body(a_ref, b_ref, out_ref):
        out_ref[rows_at(side(axis, step), count), :] = a_ref[...]
        out_ref[rows_at(1 - side(axis, step), count), :] = b_ref[...]

    return call(body, [(2 * count, mine.shape[1])], [mine, came], 8)[0]


def advanced(at, keep, came, one, tail):
    if at == 0:
        return *fold(keep, came, one, 1, tail), None
    if at == 4:
        value = unfold(keep, came, one, 1)
        return value, value, None
    value, *rest = add(keep, came, tail if at == 3 else 0)
    return value, value, *(rest or [None])


def summed_both(first, second, tail):
    states, tails = [first, second], (0, tail)
    axes = (("x", "z"), ("z", "x"))
    came = [along(axes[i][0], 0, states[i][1]) for i in range(2)]
    for at in range(5):
        for i in range(2):
            arrived, _ = lax.optimization_barrier((came[i], states[1 - i][1]))
            *states[i], rest = advanced(at, states[i][0], arrived, axes[i][0], tails[i])
            one, two = axes[i]
            came[i] = along(*((one, 1), (two, 0), (two, 1), (one, 1), (one, 0))[at], states[i][1])
            if rest is not None:
                last = rest
    return (states[0][0], came[0]), (states[1][0], came[1]), last


def inverse_factor(tail, rank):
    deep, delays = tail.shape[0], tail.shape[1] // rank
    panel = 16

    def body(tail_ref, out_ref, left_ref, right_ref):
        for d in range(delays):
            left_ref[d * deep : (d + 1) * deep, :] = tail_ref[:, d * rank : (d + 1) * rank]
        square = (rank, rank)
        same = lax.broadcasted_iota(jnp.int32, square, 0) == lax.broadcasted_iota(jnp.int32, square, 1)
        right_ref[...] = jnp.where(same, 1.0, 0.0)
        row = lax.broadcasted_iota(jnp.int32, (panel, rank), 0)
        for top in range(0, rank, panel):
            end = top + panel
            left, right = left_ref[top:end, :], right_ref[top:end, :]
            columns = [jnp.broadcast_to(left[:, top + m : top + m + 1], (panel, rank)) for m in range(panel)]
            pivots = jnp.zeros((panel, rank), F32)
            for j in range(panel):
                reciprocal = 1.0 / columns[j][j : j + 1, :]
                pivots = jnp.where(row == j, reciprocal, pivots)
                factor = jnp.where(row > j, columns[j] * reciprocal, 0.0)
                for m in range(j + 1, panel):
                    columns[m] = columns[m] - factor * columns[m][j : j + 1, :]
                left = left - factor * left[j : j + 1, :]
                right = right - factor * right[j : j + 1, :]
            if end < rank:
                factors = (left * pivots).T
                below_left, below_right = left_ref[end:, :], right_ref[end:, :]
                for j in range(panel):
                    factor = factors[end:, j : j + 1]
                    below_left = below_left - factor * left[j : j + 1, :]
                    below_right = below_right - factor * right[j : j + 1, :]
                left_ref[end:, :] = below_left
                right_ref[end:, :] = below_right
            out_ref[top:end, :] = right * lax.sqrt(pivots)

    return pl.pallas_call(
        body,
        out_shape=jax.ShapeDtypeStruct((rank, rank), F32),
        in_specs=whole(1),
        out_specs=whole(1)[0],
        scratch_shapes=[pltpu.VMEM((rank, rank), F32)] * 2,
        compiler_params=pltpu.CompilerParams(vmem_limit_bytes=8 * MIB),
    )(tail)


def shards(samples, omega):
    delays, channels, rank = omega.shape
    block = samples.shape[1]
    margin = (delays - 1) * LAG
    inner = block - margin
    width = margin + block
    half, quarter = rank // 2, rank // 4
    total = block * SIDE * SIDE

    keep, send = sketch_partial(samples, omega)
    came = lax.ppermute(send, "core", [(0, 1), (1, 0)])

    def add_cores(a_ref, b_ref, *outs):
        which = side("y", 0)
        for to, place in ((0, which), (1, 1 - which)):
            at = rows_at(place, quarter)
            outs[to][:, :margin] = a_ref[at, :margin] + b_ref[at, :margin]
            outs[to][:, margin:] = a_ref[at, block:] + b_ref[at, block:]
            outs[2 + to][...] = a_ref[at, margin:block] + b_ref[at, margin:block]

    shapes = [(quarter, 2 * margin)] * 2 + [(quarter, inner)] * 2
    ends, ends_send, middle, middle_send = call(add_cores, shapes, [keep, came], 12)
    ends_came = along("y", 0, ends_send)
    middle_came = along("y", 0, middle_send)
    (ends,) = add(ends, ends_came)
    ends_came = along("y", 1, ends)
    (middle,) = add(middle, middle_came)
    middle_came = along("y", 1, middle)

    def add_ends(a_ref, b_ref, left_ref, right_ref):
        left_ref[...] = a_ref[:, :margin] + b_ref[:, :margin]
        right_ref[...] = a_ref[:, margin:] + b_ref[:, margin:]

    left, right = call(add_ends, [(quarter, margin)] * 2, [ends, ends_came], 8)
    left_came = along("y", None, right, 1)
    right_came = along("y", None, left, -1)

    def join(left_ref, left_came_ref, right_ref, right_came_ref, middle_ref, middle_came_ref, out_ref):
        inside = lax.axis_index("x") + lax.axis_index("z") > 0
        out_ref[:, :margin] = jnp.where(inside, left_ref[...] + left_came_ref[...], 0.0)
        out_ref[:, margin:block] = middle_ref[...] + middle_came_ref[...]
        out_ref[:, block:] = right_ref[...] + right_came_ref[...]

    (mine,) = call(join, [(quarter, width)], [left, left_came, right, right_came, middle, middle_came], 8)
    sketches = [(mine, lax.ppermute(mine, "core", [(0, 1), (1, 0)]))]
    mine = along("y", 0, mine)

    first = projection_partial(samples, sketches, delays, "x", False)
    mine, *first = lax.optimization_barrier((mine, *first))
    sketches.append((mine, lax.ppermute(mine, "core", [(0, 1), (1, 0)])))
    second = projection_partial(samples, sketches, delays, "z", True)
    first, second, gram = summed_both(first, second, rank // 2)
    inverse = inverse_factor(gram, rank)

    def multiplied(turned_ref, part, places, refs, add_to):
        pick = [turned_ref[rows_at(q, quarter), :] for q in in_order(quarters()[2 * part : 2 * part + 2])]
        none = [jnp.zeros((half, rank), F32)]
        pick = [split(jnp.concatenate(m, 0)) for m in (pick + none, none + pick)]
        for place, ref in zip(places, refs):
            for pair in range(delays // 2):
                a_high, a_low = split(ref[:, pair * rank : (pair + 1) * rank])
                for odd in range(2):
                    add_to(2 * pair + odd, rows_at(place, channels // 2), dot3(a_high, a_low, *pick[odd], NN))

    def finish_first(inverse_ref, *refs):
        rows, ins, (basis_ref, out_ref, turned_ref, sketch_ref) = refs[:4], refs[4:7], refs[7:]
        turned_ref[...] = inverse_ref[...].T

        def put(d, at, value):
            out_ref[d, at, :] = value

        def put_more(d, at, value):
            out_ref[d, at, :] += value

        which = side("x", 0)
        multiplied(turned_ref, 0, (which, 1 - which), ins[:2], put)
        multiplied(turned_ref, 1, (side("z", 0),), ins[2:], put_more)
        core, y = lax.axis_index("core"), lax.axis_index("y")
        columns = block // 8
        at = pl.ds(pl.multiple_of(margin + (y * 2 + core) * columns, columns), columns)
        for place, ref in zip(quarters(), rows):
            sketch_ref[rows_at(place, quarter), :] = ref[:, at]
        high, low = split(inverse_ref[...])
        s_high, s_low = split(sketch_ref[...])
        basis_ref[...] = math.sqrt(total) * dot3(high, low, s_high, s_low, NN)

    shape = (delays, channels, rank)
    basis, partial, turned = call(
        finish_first,
        [(rank, block // 8), shape, (rank, rank)],
        [inverse, *sketches[0], *sketches[1], *first, second[0]],
        24,
        [(rank, block // 8)],
    )

    def finish_second(turned_ref, partial_ref, came_ref, out_ref):
        def put(d, at, value):
            out_ref[d, at, :] = partial_ref[d, at, :] + value

        place = 1 - side("z", 0)
        multiplied(turned_ref, 1, (place,), (came_ref,), put)
        at = rows_at(1 - place, channels // 2)
        for d in range(delays):
            out_ref[d, at, :] = partial_ref[d, at, :]

    (projection,) = call(finish_second, [shape], [turned, partial, second[1]], 24)
    return basis, projection


def solution(mesh):
    fine = Mesh(mesh.devices.reshape(SIDE, SIDE, SIDE, 2), AXES)
    tm, chan = ("x", "z"), ("y", "core")
    return jax.shard_map(
        shards,
        mesh=fine,
        in_specs=(P(chan, tm), P(None, chan, None)),
        out_specs=(P(None, tm + chan), P(None, chan, None)),
        check_vma=False,
    )
```

```python
import functools
import math

import jax
import jax.numpy as jnp
from jax import lax
from jax.experimental import pallas as pl
from jax.experimental.pallas import tpu as pltpu
from jax.sharding import Mesh
from jax.sharding import PartitionSpec as P

LAG = 512
WIDE = 1024
AHEAD = 3
F32 = jnp.float32
BF16 = jnp.bfloat16
NT = (((1,), (1,)), ((), ()))
NN = (((1,), (0,)), ((), ()))
MIB = 1024 * 1024
WEIGHT = int(2e10)


def split(value):
    high = value.astype(BF16)
    return high, (value - high.astype(F32)).astype(BF16)


def dot3(a_high, a_low, b_high, b_low, dims):
    dot = functools.partial(lax.dot_general, dimension_numbers=dims, preferred_element_type=F32)
    return dot(a_high, b_high) + (dot(a_high, b_low) + dot(a_low, b_high))


def whole(count):
    return [pl.BlockSpec(memory_space=pltpu.VMEM)] * count


def call(body, outs, args, limit=24, scratch=(), weight=0):
    return pl.pallas_call(
        body,
        out_shape=[jax.ShapeDtypeStruct(shape, F32) for shape in outs],
        in_specs=whole(len(args)),
        out_specs=whole(len(outs)),
        scratch_shapes=[pltpu.VMEM(shape, F32) for shape in scratch],
        compiler_params=pltpu.CompilerParams(vmem_limit_bytes=limit * MIB),
        cost_estimate=pl.CostEstimate(flops=weight, bytes_accessed=0, transcendentals=0) if weight else None,
    )(*args)


AXES = ("x", "z", "y", "core")
SIDE = 4


def along(axis, step, value, blocks=0):
    pairs = []
    for x in range(SIDE):
        for z in range(SIDE):
            for y in range(SIDE):
                for core in range(2):
                    flip = 0 if step is None else (1, 3)[step ^ core]
                    there = {"x": x, "z": z, "y": y}
                    there[axis] ^= flip
                    time = there["x"] * SIDE + there["z"] + blocks
                    if 0 <= time < SIDE * SIDE:
                        pairs.append((index(x, z, y, core), index(time // SIDE, time % SIDE, there["y"], core)))
    return lax.ppermute(value, AXES, pairs)


def index(x, z, y, core):
    return ((x * SIDE + z) * SIDE + y) * 2 + core


def side(axis, step, core=None):
    place = lax.axis_index(axis)
    upper = place // 2
    even = lax.rem(place + upper, 2)
    core = lax.axis_index("core") if core is None else core
    return even + (upper - even) * core if step == 0 else upper + (even - upper) * core


def rows_at(which, count):
    return pl.ds(pl.multiple_of(which * count, count), count)


def sketch_partial(samples, omega):
    delays, channels, rank = omega.shape
    block = samples.shape[1]
    steps = block // LAG
    margin = (delays - 1) * LAG
    half = rank // 2

    def body(s_hbm, o_hbm, keep_ref, send_ref, s_ref, o_ref, high_ref, low_ref, acc_ref, s_sem, o_sem):
        def fetch(step):
            at = pl.ds(pl.multiple_of(step * LAG, LAG), LAG)
            return pltpu.make_async_copy(s_hbm.at[:, at], s_ref.at[:, at], s_sem.at[step])

        fetch_omega = pltpu.make_async_copy(o_hbm, o_ref, o_sem)
        fetch_omega.start()
        fetch(0).start()
        acc_ref[...] = jnp.zeros_like(acc_ref)
        fetch_omega.wait()
        for step in range(1, AHEAD):
            fetch(step).start()
        for d in range(delays):
            high, low = split(o_ref[d].T)
            high_ref[d * rank : (d + 1) * rank, :] = high
            low_ref[d * rank : (d + 1) * rank, :] = low

        @pl.loop(0, steps)
        def _(step):
            fetch(step).wait()

            @pl.when(step + AHEAD < steps)
            def _():
                fetch(step + AHEAD).start()

            s_high, s_low = split(s_ref[:, pl.ds(pl.multiple_of(step * LAG, LAG), LAG)])
            term = dot3(high_ref[...], low_ref[...], s_high, s_low, NN)
            for d in range(delays):
                at = pl.ds(pl.multiple_of((step + delays - 1 - d) * LAG, LAG), LAG)
                acc_ref[:, at] += term[d * rank : (d + 1) * rank, :]

        core = lax.axis_index("core")
        keep_ref[...] = acc_ref[rows_at(core, half), :]
        send_ref[...] = acc_ref[rows_at(1 - core, half), :]

    out = jax.ShapeDtypeStruct((half, margin + block), F32)
    return pl.pallas_call(
        body,
        out_shape=[out, out, pltpu.VMEM(samples.shape, F32)],
        in_specs=[pl.BlockSpec(memory_space=pltpu.HBM)] * 2,
        out_specs=whole(3),
        scratch_shapes=[
            pltpu.VMEM(omega.shape, F32),
            pltpu.VMEM((delays * rank, channels), BF16),
            pltpu.VMEM((delays * rank, channels), BF16),
            pltpu.VMEM((rank, margin + block), F32),
            pltpu.SemaphoreType.DMA((steps,)),
            pltpu.SemaphoreType.DMA,
        ],
        compiler_params=pltpu.CompilerParams(vmem_limit_bytes=20 * MIB),
        cost_estimate=pl.CostEstimate(
            flops=6 * delays * rank * channels * block, bytes_accessed=samples.size * 4, transcendentals=0
        ),
    )(samples, pltpu.with_memory_space_constraint(omega, pltpu.HBM))


def quarters():
    core = lax.axis_index("core")
    own, other = side("y", 0), side("y", 0, 1 - core)
    return [2 * core + own, 2 * (1 - core) + other, 2 * core + 1 - own, 2 * (1 - core) + 1 - other]


def in_order(places):
    return jnp.minimum(*places), jnp.maximum(*places)


def projection_partial(samples, sketch, delays, axis):
    channels, block = samples.shape
    quarter, width = sketch[0].shape
    count = 2 * quarter
    steps = block // WIDE
    lanes = delays * count

    def body(s_ref, mine_ref, other_ref, keep_ref, send_ref, high_ref, low_ref, acc_ref):
        core = lax.axis_index("core")
        for place, ref in ((core, mine_ref), (1 - core, other_ref)):
            high, low = split(ref[...])
            high_ref[rows_at(place, quarter), :] = high
            low_ref[rows_at(place, quarter), :] = low
        acc_ref[...] = jnp.zeros_like(acc_ref)

        @pl.loop(0, steps)
        def _(step):
            s_high, s_low = split(s_ref[:, pl.ds(pl.multiple_of(step * WIDE, WIDE), WIDE)])
            highs, lows = [], []
            for d in range(delays):
                at = pl.ds(pl.multiple_of(step * WIDE + (delays - 1 - d) * LAG, LAG), WIDE)
                highs.append(high_ref[:, at])
                lows.append(low_ref[:, at])
            acc_ref[...] += dot3(s_high, s_low, jnp.concatenate(highs, 0), jnp.concatenate(lows, 0), NT)

        which = side(axis, 0)
        for place, ref in ((which, keep_ref), (1 - which, send_ref)):
            ref[...] = acc_ref[rows_at(place, channels // 2), :]

    return pl.pallas_call(
        body,
        out_shape=[jax.ShapeDtypeStruct((channels // 2, lanes), F32)] * 2,
        in_specs=whole(3),
        out_specs=whole(2),
        scratch_shapes=[
            pltpu.VMEM((count, width), BF16),
            pltpu.VMEM((count, width), BF16),
            pltpu.VMEM((channels, lanes), F32),
        ],
        compiler_params=pltpu.CompilerParams(vmem_limit_bytes=24 * MIB),
        cost_estimate=pl.CostEstimate(flops=4 * WEIGHT, bytes_accessed=channels * block * 4, transcendentals=0),
    )(samples, *sketch)


def with_gram(keep, send, sketches, margin):
    quarter, width = sketches[0][0].shape
    rank = 4 * quarter
    rows, lanes = keep.shape
    tail = rank * rank // lanes

    def body(keep_ref, send_ref, *refs):
        ins, outs, (sketch_ref, gram_ref) = refs[:4], refs[4:6], refs[6:]
        for place, ref in zip(quarters(), ins):
            sketch_ref[rows_at(place, quarter), :] = ref[:, margin:]
        high, low = split(sketch_ref[...])
        gram_ref[...] = dot3(high, low, high, low, NT)
        for ref, out_ref in zip((keep_ref, send_ref), outs):
            out_ref[:rows, :] = ref[...]
            for group in range(lanes // rank):
                out_ref[rows:, group * rank : (group + 1) * rank] = gram_ref[group * tail : (group + 1) * tail, :]

    flat = [half for pair in sketches for half in pair]
    shapes = [(rows + tail, lanes)] * 2
    return call(body, shapes, [keep, send, *flat], 16, [(rank, width - margin), (rank, rank)])


def fold(keep, came, axis, step, tail=0):
    count = (keep.shape[0] - tail) // 2

    def body(a_ref, b_ref, keep_ref, send_ref):
        which = side(axis, step)
        for place, ref in ((which, keep_ref), (1 - which, send_ref)):
            at = rows_at(place, count)
            ref[:count, :] = a_ref[at, :] + b_ref[at, :]
            if tail:
                ref[count:, :] = a_ref[2 * count :, :] + b_ref[2 * count :, :]

    return call(body, [(count + tail, keep.shape[1])] * 2, [keep, came], 8, weight=WEIGHT)


def add(a, b, tail=0):
    count = a.shape[0] - tail

    def body(a_ref, b_ref, out_ref, *tails):
        out_ref[...] = a_ref[:count, :] + b_ref[:count, :]
        for ref in tails:
            ref[...] = a_ref[count:, :] + b_ref[count:, :]

    return call(body, [(count, a.shape[1])] + [(tail, a.shape[1])] * (tail > 0), [a, b], 8, weight=WEIGHT)


def unfold(mine, came, axis, step):
    count = mine.shape[0]

    def body(a_ref, b_ref, out_ref):
        out_ref[rows_at(side(axis, step), count), :] = a_ref[...]
        out_ref[rows_at(1 - side(axis, step), count), :] = b_ref[...]

    return call(body, [(2 * count, mine.shape[1])], [mine, came], 8, weight=WEIGHT)[0]


def advanced(at, keep, came, one, tail):
    if at == 0:
        return *fold(keep, came, one, 1, tail), None
    if at == 4:
        value = unfold(keep, came, one, 1)
        return value, value, None
    value, *rest = add(keep, came, tail if at == 3 else 0)
    return value, value, *(rest or [None])


def summed_both(first, second, tail):
    states, tails = [first, second], (tail, 0)
    axes = (("x", "z"), ("z", "x"))
    came = [along(axes[i][0], 0, states[i][1]) for i in range(2)]
    for at in range(5):
        for i in range(2):
            arrived, _ = lax.optimization_barrier((came[i], states[1 - i][1]))
            *states[i], rest = advanced(at, states[i][0], arrived, axes[i][0], tails[i])
            one, two = axes[i]
            came[i] = along(*((one, 1), (two, 0), (two, 1), (one, 1), (one, 0))[at], states[i][1])
            if rest is not None:
                last = rest
    return (states[0][0], came[0]), (states[1][0], came[1]), last


def inverse_factor(tail, rank):
    deep, delays = tail.shape[0], tail.shape[1] // rank
    panel = 16

    def body(tail_ref, out_ref, left_ref, right_ref):
        for d in range(delays):
            left_ref[d * deep : (d + 1) * deep, :] = tail_ref[:, d * rank : (d + 1) * rank]
        square = (rank, rank)
        same = lax.broadcasted_iota(jnp.int32, square, 0) == lax.broadcasted_iota(jnp.int32, square, 1)
        right_ref[...] = jnp.where(same, 1.0, 0.0)
        row = lax.broadcasted_iota(jnp.int32, (panel, rank), 0)
        for top in range(0, rank, panel):
            end = top + panel
            left, right = left_ref[top:end, :], right_ref[top:end, :]
            columns = [jnp.broadcast_to(left[:, top + m : top + m + 1], (panel, rank)) for m in range(panel)]
            pivots = jnp.zeros((panel, rank), F32)
            for j in range(panel):
                reciprocal = 1.0 / columns[j][j : j + 1, :]
                pivots = jnp.where(row == j, reciprocal, pivots)
                factor = jnp.where(row > j, columns[j] * reciprocal, 0.0)
                for m in range(j + 1, panel):
                    columns[m] = columns[m] - factor * columns[m][j : j + 1, :]
                left = left - factor * left[j : j + 1, :]
                right = right - factor * right[j : j + 1, :]
            if end < rank:
                factors = (left * pivots).T
                below_left, below_right = left_ref[end:, :], right_ref[end:, :]
                for j in range(panel):
                    factor = factors[end:, j : j + 1]
                    below_left = below_left - factor * left[j : j + 1, :]
                    below_right = below_right - factor * right[j : j + 1, :]
                left_ref[end:, :] = below_left
                right_ref[end:, :] = below_right
            out_ref[top:end, :] = right * lax.sqrt(pivots)

    return pl.pallas_call(
        body,
        out_shape=jax.ShapeDtypeStruct((rank, rank), F32),
        in_specs=whole(1),
        out_specs=whole(1)[0],
        scratch_shapes=[pltpu.VMEM((rank, rank), F32)] * 2,
        compiler_params=pltpu.CompilerParams(vmem_limit_bytes=8 * MIB),
    )(tail)


def shards(samples, omega):
    delays, channels, rank = omega.shape
    block = samples.shape[1]
    margin = (delays - 1) * LAG
    inner = block - margin
    width = margin + block
    half, quarter = rank // 2, rank // 4
    total = block * SIDE * SIDE

    keep, send, samples = sketch_partial(samples, omega)
    came = lax.ppermute(send, "core", [(0, 1), (1, 0)])

    def add_cores(a_ref, b_ref, *outs):
        which = side("y", 0)
        for to, place in ((0, which), (1, 1 - which)):
            at = rows_at(place, quarter)
            outs[to][:, :margin] = a_ref[at, :margin] + b_ref[at, :margin]
            outs[to][:, margin:] = a_ref[at, block:] + b_ref[at, block:]
            outs[2 + to][...] = a_ref[at, margin:block] + b_ref[at, margin:block]

    shapes = [(quarter, 2 * margin)] * 2 + [(quarter, inner)] * 2
    ends, ends_send, middle, middle_send = call(add_cores, shapes, [keep, came], 12)
    ends_came = along("y", 0, ends_send)
    middle_came = along("y", 0, middle_send)
    (ends,) = add(ends, ends_came)
    ends_came = along("y", 1, ends)
    (middle,) = add(middle, middle_came)
    middle_came = along("y", 1, middle)

    def add_ends(a_ref, b_ref, left_ref, right_ref):
        left_ref[...] = a_ref[:, :margin] + b_ref[:, :margin]
        right_ref[...] = a_ref[:, margin:] + b_ref[:, margin:]

    left, right = call(add_ends, [(quarter, margin)] * 2, [ends, ends_came], 8)
    left_came = along("y", None, right, 1)
    right_came = along("y", None, left, -1)

    def join(left_ref, left_came_ref, right_ref, right_came_ref, middle_ref, middle_came_ref, out_ref):
        inside = lax.axis_index("x") + lax.axis_index("z") > 0
        out_ref[:, :margin] = jnp.where(inside, left_ref[...] + left_came_ref[...], 0.0)
        out_ref[:, margin:block] = middle_ref[...] + middle_came_ref[...]
        out_ref[:, block:] = right_ref[...] + right_came_ref[...]

    (mine,) = call(join, [(quarter, width)], [left, left_came, right, right_came, middle, middle_came], 8)
    sketches = [(mine, lax.ppermute(mine, "core", [(0, 1), (1, 0)]))]
    mine = along("y", 0, mine)

    first = projection_partial(samples, sketches[0], delays, "x")
    mine, *first = lax.optimization_barrier((mine, *first))
    sketches.append((mine, lax.ppermute(mine, "core", [(0, 1), (1, 0)])))
    first = with_gram(*first, sketches, margin)
    second = projection_partial(samples, sketches[1], delays, "z")
    first, second, gram = summed_both(first, second, rank // 2)
    inverse = inverse_factor(gram, rank)

    def multiplied(turned_ref, part, places, refs, add_to):
        pick = [turned_ref[rows_at(q, quarter), :] for q in in_order(quarters()[2 * part : 2 * part + 2])]
        none = [jnp.zeros((half, rank), F32)]
        pick = [split(jnp.concatenate(m, 0)) for m in (pick + none, none + pick)]
        for place, ref in zip(places, refs):
            for pair in range(delays // 2):
                a_high, a_low = split(ref[:, pair * rank : (pair + 1) * rank])
                for odd in range(2):
                    add_to(2 * pair + odd, rows_at(place, channels // 2), dot3(a_high, a_low, *pick[odd], NN))

    def finish_first(inverse_ref, *refs):
        rows, ins, (basis_ref, out_ref, turned_ref, sketch_ref) = refs[:4], refs[4:7], refs[7:]
        turned_ref[...] = inverse_ref[...].T

        def put(d, at, value):
            out_ref[d, at, :] = value

        def put_more(d, at, value):
            out_ref[d, at, :] += value

        which = side("x", 0)
        multiplied(turned_ref, 0, (which, 1 - which), ins[:2], put)
        multiplied(turned_ref, 1, (side("z", 0),), ins[2:], put_more)
        core, y = lax.axis_index("core"), lax.axis_index("y")
        columns = block // 8
        at = pl.ds(pl.multiple_of(margin + (y * 2 + core) * columns, columns), columns)
        for place, ref in zip(quarters(), rows):
            sketch_ref[rows_at(place, quarter), :] = ref[:, at]
        high, low = split(inverse_ref[...])
        s_high, s_low = split(sketch_ref[...])
        basis_ref[...] = math.sqrt(total) * dot3(high, low, s_high, s_low, NN)

    shape = (delays, channels, rank)
    basis, partial, turned = call(
        finish_first,
        [(rank, block // 8), shape, (rank, rank)],
        [inverse, *sketches[0], *sketches[1], *first, second[0]],
        24,
        [(rank, block // 8)],
    )

    def finish_second(turned_ref, partial_ref, came_ref, out_ref):
        def put(d, at, value):
            out_ref[d, at, :] = partial_ref[d, at, :] + value

        place = 1 - side("z", 0)
        multiplied(turned_ref, 1, (place,), (came_ref,), put)
        at = rows_at(1 - place, channels // 2)
        for d in range(delays):
            out_ref[d, at, :] = partial_ref[d, at, :]

    (projection,) = call(finish_second, [shape], [turned, partial, second[1]], 24)
    return basis, projection


def solution(mesh):
    fine = Mesh(mesh.devices.reshape(SIDE, SIDE, SIDE, 2), AXES)
    tm, chan = ("x", "z"), ("y", "core")
    return jax.shard_map(
        shards,
        mesh=fine,
        in_specs=(P(chan, tm), P(None, chan, None)),
        out_specs=(P(None, tm + chan), P(None, chan, None)),
        check_vma=False,
    )
```

```python
import functools
import math

import jax
import jax.numpy as jnp
from jax import lax
from jax.experimental import pallas as pl
from jax.experimental.pallas import tpu as pltpu
from jax.sharding import Mesh
from jax.sharding import PartitionSpec as P

LAG = 512
WIDE = 1024
AHEAD = 3
F32 = jnp.float32
BF16 = jnp.bfloat16
NT = (((1,), (1,)), ((), ()))
NN = (((1,), (0,)), ((), ()))
MIB = 1024 * 1024
WEIGHT = int(2e10)


def split(value):
    high = value.astype(BF16)
    return high, (value - high.astype(F32)).astype(BF16)


def dot3(a_high, a_low, b_high, b_low, dims):
    dot = functools.partial(lax.dot_general, dimension_numbers=dims, preferred_element_type=F32)
    return dot(a_high, b_high) + (dot(a_high, b_low) + dot(a_low, b_high))


def whole(count):
    return [pl.BlockSpec(memory_space=pltpu.VMEM)] * count


def call(body, outs, args, limit=24, scratch=(), weight=0):
    return pl.pallas_call(
        body,
        out_shape=[jax.ShapeDtypeStruct(shape, F32) for shape in outs],
        in_specs=whole(len(args)),
        out_specs=whole(len(outs)),
        scratch_shapes=[pltpu.VMEM(shape, F32) for shape in scratch],
        compiler_params=pltpu.CompilerParams(vmem_limit_bytes=limit * MIB),
        cost_estimate=pl.CostEstimate(flops=weight, bytes_accessed=0, transcendentals=0) if weight else None,
    )(*args)


AXES = ("x", "z", "y", "core")
SIDE = 4


def along(axis, step, value, blocks=0):
    pairs = []
    for x in range(SIDE):
        for z in range(SIDE):
            for y in range(SIDE):
                for core in range(2):
                    flip = 0 if step is None else (1, 3)[step ^ core]
                    there = {"x": x, "z": z, "y": y}
                    there[axis] ^= flip
                    time = there["x"] * SIDE + there["z"] + blocks
                    if 0 <= time < SIDE * SIDE:
                        pairs.append((index(x, z, y, core), index(time // SIDE, time % SIDE, there["y"], core)))
    return lax.ppermute(value, AXES, pairs)


def index(x, z, y, core):
    return ((x * SIDE + z) * SIDE + y) * 2 + core


def side(axis, step, core=None):
    place = lax.axis_index(axis)
    upper = place // 2
    even = lax.rem(place + upper, 2)
    core = lax.axis_index("core") if core is None else core
    return even + (upper - even) * core if step == 0 else upper + (even - upper) * core


def rows_at(which, count):
    return pl.ds(pl.multiple_of(which * count, count), count)


def sketch_ends(samples, omega):
    delays, channels, rank = omega.shape
    block = samples.shape[1]
    steps = block // LAG
    reach = delays - 1
    margin, half = reach * LAG, rank // 2
    edge = 2 * reach

    def place(at):
        inner = steps - edge
        moved = jnp.where(at < edge, at + inner, at - reach)
        return jnp.where(at < reach, at, moved)

    def body(s_hbm, o_hbm, keep_ref, send_ref, middle_ref, s_ref, high_ref, low_ref, o_ref, acc_ref, s_sem, o_sem):
        def fetch(at):
            columns = pl.ds(pl.multiple_of(place(at) * LAG, LAG), LAG)
            return pltpu.make_async_copy(s_hbm.at[:, columns], s_ref.at[:, columns], s_sem.at[at])

        fetch_omega = pltpu.make_async_copy(o_hbm, o_ref, o_sem)
        fetch_omega.start()
        fetch(0).start()
        acc_ref[...] = jnp.zeros_like(acc_ref)
        fetch_omega.wait()
        for at in range(1, AHEAD):
            fetch(at).start()
        for d in range(delays):
            high, low = split(o_ref[d].T)
            high_ref[d * rank : (d + 1) * rank, :] = high
            low_ref[d * rank : (d + 1) * rank, :] = low

        @pl.loop(0, edge)
        def _(at):
            fetch(at).wait()

            @pl.when(at + AHEAD < steps)
            def _():
                fetch(at + AHEAD).start()

            s_high, s_low = split(s_ref[:, pl.ds(pl.multiple_of(place(at) * LAG, LAG), LAG)])
            term = dot3(high_ref[...], low_ref[...], s_high, s_low, NN)
            for d in range(delays):
                to = pl.ds(pl.multiple_of((place(at) + reach - d) * LAG, LAG), LAG)
                acc_ref[:, to] += term[d * rank : (d + 1) * rank, :]

        for at in range(edge, steps):
            if at >= edge + AHEAD:
                fetch(at).start()
            fetch(at).wait()
        core = lax.axis_index("core")
        for which, ref in ((core, keep_ref), (1 - core, send_ref)):
            ref[:, :margin] = acc_ref[rows_at(which, half), :margin]
            ref[:, margin:] = acc_ref[rows_at(which, half), block:]
        middle_ref[...] = acc_ref[:, margin:block]

    ends = jax.ShapeDtypeStruct((half, 2 * margin), F32)
    return pl.pallas_call(
        body,
        out_shape=[
            ends,
            ends,
            jax.ShapeDtypeStruct((rank, block - margin), F32),
            pltpu.VMEM(samples.shape, F32),
            jax.ShapeDtypeStruct((delays * rank, channels), BF16),
            jax.ShapeDtypeStruct((delays * rank, channels), BF16),
        ],
        in_specs=[pl.BlockSpec(memory_space=pltpu.HBM)] * 2,
        out_specs=whole(6),
        scratch_shapes=[
            pltpu.VMEM(omega.shape, F32),
            pltpu.VMEM((rank, margin + block), F32),
            pltpu.SemaphoreType.DMA((steps,)),
            pltpu.SemaphoreType.DMA,
        ],
        compiler_params=pltpu.CompilerParams(vmem_limit_bytes=20 * MIB),
        cost_estimate=pl.CostEstimate(flops=4 * WEIGHT, bytes_accessed=samples.size * 4, transcendentals=0),
    )(samples, pltpu.with_memory_space_constraint(omega, pltpu.HBM))


def sketch_middle(middle, samples, high, low, delays):
    rank, inner = middle.shape
    block = samples.shape[1]
    reach = delays - 1
    half = rank // 2

    def body(middle_ref, s_ref, high_ref, low_ref, keep_ref, send_ref, acc_ref):
        acc_ref[...] = middle_ref[...]
        for step in range(reach, block // LAG - reach):
            s_high, s_low = split(s_ref[:, step * LAG : (step + 1) * LAG])
            term = dot3(high_ref[...], low_ref[...], s_high, s_low, NN)
            for d in range(delays):
                acc_ref[:, (step - d) * LAG : (step - d + 1) * LAG] += term[d * rank : (d + 1) * rank, :]
        core = lax.axis_index("core")
        for which, ref in ((core, keep_ref), (1 - core, send_ref)):
            ref[...] = acc_ref[rows_at(which, half), :]

    return call(
        body, [(half, inner)] * 2, [middle, samples, high, low], 16, [(rank, inner)], weight=2 * WEIGHT
    )


def quarters():
    core = lax.axis_index("core")
    own, other = side("y", 0), side("y", 0, 1 - core)
    return [2 * core + own, 2 * (1 - core) + other, 2 * core + 1 - own, 2 * (1 - core) + 1 - other]


def in_order(places):
    return jnp.minimum(*places), jnp.maximum(*places)


def projection_partial(samples, sketch, delays, axis):
    channels, block = samples.shape
    quarter, width = sketch[0].shape
    count = 2 * quarter
    steps = block // WIDE
    lanes = delays * count

    def body(s_ref, mine_ref, other_ref, keep_ref, send_ref, high_ref, low_ref, acc_ref):
        core = lax.axis_index("core")
        for place, ref in ((core, mine_ref), (1 - core, other_ref)):
            high, low = split(ref[...])
            high_ref[rows_at(place, quarter), :] = high
            low_ref[rows_at(place, quarter), :] = low
        acc_ref[...] = jnp.zeros_like(acc_ref)

        @pl.loop(0, steps)
        def _(step):
            s_high, s_low = split(s_ref[:, pl.ds(pl.multiple_of(step * WIDE, WIDE), WIDE)])
            highs, lows = [], []
            for d in range(delays):
                at = pl.ds(pl.multiple_of(step * WIDE + (delays - 1 - d) * LAG, LAG), WIDE)
                highs.append(high_ref[:, at])
                lows.append(low_ref[:, at])
            acc_ref[...] += dot3(s_high, s_low, jnp.concatenate(highs, 0), jnp.concatenate(lows, 0), NT)

        which = side(axis, 0)
        for place, ref in ((which, keep_ref), (1 - which, send_ref)):
            ref[...] = acc_ref[rows_at(place, channels // 2), :]

    return pl.pallas_call(
        body,
        out_shape=[jax.ShapeDtypeStruct((channels // 2, lanes), F32)] * 2,
        in_specs=whole(3),
        out_specs=whole(2),
        scratch_shapes=[
            pltpu.VMEM((count, width), BF16),
            pltpu.VMEM((count, width), BF16),
            pltpu.VMEM((channels, lanes), F32),
        ],
        compiler_params=pltpu.CompilerParams(vmem_limit_bytes=24 * MIB),
        cost_estimate=pl.CostEstimate(flops=4 * WEIGHT, bytes_accessed=channels * block * 4, transcendentals=0),
    )(samples, *sketch)


def fold_with_gram(keep, came, axis, step, sketches, margin):
    quarter, width = sketches[0][0].shape
    rank = 4 * quarter
    count, lanes = keep.shape[0] // 2, keep.shape[1]
    tail = rank * rank // lanes

    def body(a_ref, b_ref, *refs):
        ins, outs, (sketch_ref, gram_ref) = refs[:4], refs[4:6], refs[6:]
        for place, ref in zip(quarters(), ins):
            sketch_ref[rows_at(place, quarter), :] = ref[:, margin:]
        high, low = split(sketch_ref[...])
        gram_ref[...] = dot3(high, low, high, low, NT)
        which = side(axis, step)
        for place, ref in zip((which, 1 - which), outs):
            at = rows_at(place, count)
            ref[:count, :] = a_ref[at, :] + b_ref[at, :]
            for group in range(lanes // rank):
                ref[count:, group * rank : (group + 1) * rank] = gram_ref[group * tail : (group + 1) * tail, :]

    flat = [half for pair in sketches for half in pair]
    scratch = [(rank, width - margin), (rank, rank)]
    return call(body, [(count + tail, lanes)] * 2, [keep, came, *flat], 16, scratch, weight=WEIGHT)


def fold(keep, came, axis, step):
    count = keep.shape[0] // 2

    def body(a_ref, b_ref, keep_ref, send_ref):
        which = side(axis, step)
        for place, ref in ((which, keep_ref), (1 - which, send_ref)):
            at = rows_at(place, count)
            ref[...] = a_ref[at, :] + b_ref[at, :]

    return call(body, [(count, keep.shape[1])] * 2, [keep, came], 8, weight=WEIGHT)


def add(a, b, tail=0):
    count = a.shape[0] - tail

    def body(a_ref, b_ref, out_ref, *tails):
        out_ref[...] = a_ref[:count, :] + b_ref[:count, :]
        for ref in tails:
            ref[...] = a_ref[count:, :] + b_ref[count:, :]

    return call(body, [(count, a.shape[1])] + [(tail, a.shape[1])] * (tail > 0), [a, b], 8, weight=WEIGHT)


def unfold(mine, came, axis, step):
    count = mine.shape[0]

    def body(a_ref, b_ref, out_ref):
        out_ref[rows_at(side(axis, step), count), :] = a_ref[...]
        out_ref[rows_at(1 - side(axis, step), count), :] = b_ref[...]

    return call(body, [(2 * count, mine.shape[1])], [mine, came], 8, weight=WEIGHT)[0]


def advanced(at, keep, came, one, tail):
    if at == 4:
        value = unfold(keep, came, one, 1)
        return value, value, None
    value, *rest = add(keep, came, tail if at == 3 else 0)
    return value, value, *(rest or [None])


def summed_both(first, second, sketches, margin):
    states = [first, second]
    axes = (("x", "z"), ("z", "x"))
    came = [along(axes[i][0], 0, states[i][1]) for i in range(2)]
    for at in range(5):
        for i in range(2):
            arrived, _ = lax.optimization_barrier((came[i], states[1 - i][1]))
            one, two = axes[i]
            if at > 0:
                tail = 0 if i else states[i][0].shape[0] - first[0].shape[0] // 2
                *states[i], rest = advanced(at, states[i][0], arrived, one, tail)
                if rest is not None:
                    gram = add(rest, along(one, 0, rest))[0]
            elif i == 0:
                states[i] = fold_with_gram(states[i][0], arrived, one, 1, sketches, margin)
            else:
                states[i] = fold(states[i][0], arrived, one, 1)
            came[i] = along(*((one, 1), (two, 0), (two, 1), (one, 1), (one, 0))[at], states[i][1])
    return (states[0][0], came[0]), (states[1][0], came[1]), gram


def inverse_factor(tail, rank):
    deep, delays = tail.shape[0], tail.shape[1] // rank
    panel = 16

    def body(tail_ref, out_ref, left_ref, right_ref):
        for d in range(delays):
            left_ref[d * deep : (d + 1) * deep, :] = tail_ref[:, d * rank : (d + 1) * rank]
        square = (rank, rank)
        same = lax.broadcasted_iota(jnp.int32, square, 0) == lax.broadcasted_iota(jnp.int32, square, 1)
        right_ref[...] = jnp.where(same, 1.0, 0.0)
        row = lax.broadcasted_iota(jnp.int32, (panel, rank), 0)
        for top in range(0, rank, panel):
            end = top + panel
            left, right = left_ref[top:end, :], right_ref[top:end, :]
            columns = [jnp.broadcast_to(left[:, top + m : top + m + 1], (panel, rank)) for m in range(panel)]
            pivots = jnp.zeros((panel, rank), F32)
            for j in range(panel):
                reciprocal = 1.0 / columns[j][j : j + 1, :]
                pivots = jnp.where(row == j, reciprocal, pivots)
                factor = jnp.where(row > j, columns[j] * reciprocal, 0.0)
                for m in range(j + 1, panel):
                    columns[m] = columns[m] - factor * columns[m][j : j + 1, :]
                left = left - factor * left[j : j + 1, :]
                right = right - factor * right[j : j + 1, :]
            if end < rank:
                factors = (left * pivots).T
                below_left, below_right = left_ref[end:, :], right_ref[end:, :]
                for j in range(panel):
                    factor = factors[end:, j : j + 1]
                    below_left = below_left - factor * left[j : j + 1, :]
                    below_right = below_right - factor * right[j : j + 1, :]
                left_ref[end:, :] = below_left
                right_ref[end:, :] = below_right
            out_ref[top:end, :] = right * lax.sqrt(pivots)

    return pl.pallas_call(
        body,
        out_shape=jax.ShapeDtypeStruct((rank, rank), F32),
        in_specs=whole(1),
        out_specs=whole(1)[0],
        scratch_shapes=[pltpu.VMEM((rank, rank), F32)] * 2,
        compiler_params=pltpu.CompilerParams(vmem_limit_bytes=8 * MIB),
    )(tail)


def shards(samples, omega):
    delays, channels, rank = omega.shape
    block = samples.shape[1]
    margin = (delays - 1) * LAG
    inner = block - margin
    width = margin + block
    half, quarter = rank // 2, rank // 4
    total = block * SIDE * SIDE

    ends, ends_send, middle, samples, high, low = sketch_ends(samples, omega)
    middle, middle_send = sketch_middle(middle, samples, high, low, delays)
    ends, ends_send = fold(ends, lax.ppermute(ends_send, "core", [(0, 1), (1, 0)]), "y", 0)
    middle, middle_send = fold(middle, lax.ppermute(middle_send, "core", [(0, 1), (1, 0)]), "y", 0)
    ends_came = along("y", 0, ends_send)
    middle_came = along("y", 0, middle_send)
    (ends,) = add(ends, ends_came)
    ends_came = along("y", 1, ends)
    (middle,) = add(middle, middle_came)
    middle_came = along("y", 1, middle)

    def add_ends(a_ref, b_ref, left_ref, right_ref):
        left_ref[...] = a_ref[:, :margin] + b_ref[:, :margin]
        right_ref[...] = a_ref[:, margin:] + b_ref[:, margin:]

    left, right = call(add_ends, [(quarter, margin)] * 2, [ends, ends_came], 8)
    left_came = along("y", None, right, 1)
    right_came = along("y", None, left, -1)

    def join(left_ref, left_came_ref, right_ref, right_came_ref, middle_ref, middle_came_ref, out_ref):
        inside = lax.axis_index("x") + lax.axis_index("z") > 0
        out_ref[:, :margin] = jnp.where(inside, left_ref[...] + left_came_ref[...], 0.0)
        out_ref[:, margin:block] = middle_ref[...] + middle_came_ref[...]
        out_ref[:, block:] = right_ref[...] + right_came_ref[...]

    (mine,) = call(join, [(quarter, width)], [left, left_came, right, right_came, middle, middle_came], 8)
    sketches = [(mine, lax.ppermute(mine, "core", [(0, 1), (1, 0)]))]
    mine = along("y", 0, mine)

    first = projection_partial(samples, sketches[0], delays, "x")
    mine, *first = lax.optimization_barrier((mine, *first))
    sketches.append((mine, lax.ppermute(mine, "core", [(0, 1), (1, 0)])))
    second = projection_partial(samples, sketches[1], delays, "z")
    first, second, gram = summed_both(first, second, sketches, margin)
    inverse = inverse_factor(gram, rank)

    def multiplied(turned_ref, part, ref, put):
        pick = [turned_ref[rows_at(q, quarter), :] for q in in_order(quarters()[2 * part : 2 * part + 2])]
        none = [jnp.zeros((half, rank), F32)]
        pick = [split(jnp.concatenate(m, 0)) for m in (pick + none, none + pick)]
        for pair in range(delays // 2):
            a_high, a_low = split(ref[:, pair * rank : (pair + 1) * rank])
            for odd in range(2):
                put(2 * pair + odd, dot3(a_high, a_low, *pick[odd], NN))

    def finish_first(inverse_ref, *refs):
        rows, ins, outs, (mine_ref, sketch_ref, sem, both_ref) = refs[:4], refs[4:7], refs[7:11], refs[11:]
        basis_ref, out_ref, partial_ref, turned_ref = outs
        turned_ref[...] = inverse_ref[...].T
        which = side("z", 0)
        here = side("x", 0)

        def put_first(place):
            def put(d, value):
                both_ref[d, rows_at(place, channels // 2), :] = value

            return put

        multiplied(turned_ref, 0, ins[0], put_first(here))
        multiplied(turned_ref, 0, ins[1], put_first(1 - here))

        def copy(d):
            return pltpu.make_async_copy(mine_ref.at[d], out_ref.at[d, rows_at(which, channels // 2), :], sem.at[d])

        def put_second(d, value):
            mine_ref[d] = both_ref[d, rows_at(which, channels // 2), :] + value
            copy(d).start()

        multiplied(turned_ref, 1, ins[2], put_second)
        for d in range(delays):
            partial_ref[d] = both_ref[d, rows_at(1 - which, channels // 2), :]
        core, y = lax.axis_index("core"), lax.axis_index("y")
        columns = block // 8
        at = pl.ds(pl.multiple_of(margin + (y * 2 + core) * columns, columns), columns)
        for place, ref in zip(quarters(), rows):
            sketch_ref[rows_at(place, quarter), :] = ref[:, at]
        high, low = split(inverse_ref[...])
        s_high, s_low = split(sketch_ref[...])
        basis_ref[...] = math.sqrt(total) * dot3(high, low, s_high, s_low, NN)
        for d in range(delays):
            copy(d).wait()

    shape, part_shape = (delays, channels, rank), (delays, channels // 2, rank)
    outs = [jax.ShapeDtypeStruct(s, F32) for s in ((rank, block // 8), shape, part_shape, (rank, rank))]
    basis, projection, partial, turned = pl.pallas_call(
        finish_first,
        out_shape=outs,
        in_specs=whole(8),
        out_specs=whole(1) + [pl.BlockSpec(memory_space=pltpu.HBM)] + whole(2),
        scratch_shapes=[
            pltpu.VMEM(part_shape, F32),
            pltpu.VMEM((rank, block // 8), F32),
            pltpu.SemaphoreType.DMA((delays,)),
            pltpu.VMEM(shape, F32),
        ],
        compiler_params=pltpu.CompilerParams(vmem_limit_bytes=24 * MIB),
    )(inverse, *sketches[0], *sketches[1], *first, second[0])

    def finish_second(turned_ref, partial_ref, came_ref, _, out_ref, mine_ref, sem):
        which = 1 - side("z", 0)

        def copy(d):
            return pltpu.make_async_copy(mine_ref.at[d], out_ref.at[d, rows_at(which, channels // 2), :], sem.at[d])

        def put(d, value):
            mine_ref[d] = partial_ref[d] + value
            copy(d).start()

        multiplied(turned_ref, 1, came_ref, put)
        for d in range(delays):
            copy(d).wait()

    projection = pl.pallas_call(
        finish_second,
        out_shape=outs[1],
        in_specs=whole(3) + [pl.BlockSpec(memory_space=pltpu.HBM)],
        out_specs=pl.BlockSpec(memory_space=pltpu.HBM),
        scratch_shapes=[pltpu.VMEM(part_shape, F32), pltpu.SemaphoreType.DMA((delays,))],
        input_output_aliases={3: 0},
        compiler_params=pltpu.CompilerParams(vmem_limit_bytes=16 * MIB),
    )(turned, partial, second[1], projection)
    return basis, projection


def solution(mesh):
    fine = Mesh(mesh.devices.reshape(SIDE, SIDE, SIDE, 2), AXES)
    tm, chan = ("x", "z"), ("y", "core")
    return jax.shard_map(
        shards,
        mesh=fine,
        in_specs=(P(chan, tm), P(None, chan, None)),
        out_specs=(P(None, tm + chan), P(None, chan, None)),
        check_vma=False,
    )
```

```python
import functools
import math

import jax
import jax.numpy as jnp
from jax import lax
from jax.experimental import pallas as pl
from jax.experimental.pallas import tpu as pltpu
from jax.sharding import Mesh
from jax.sharding import PartitionSpec as P

LAG = 512
WIDE = 1024
AHEAD = 3
F32 = jnp.float32
BF16 = jnp.bfloat16
NT = (((1,), (1,)), ((), ()))
NN = (((1,), (0,)), ((), ()))
MIB = 1024 * 1024
WEIGHT = int(2e10)


def split(value):
    high = value.astype(BF16)
    return high, (value - high.astype(F32)).astype(BF16)


def dot3(a_high, a_low, b_high, b_low, dims):
    dot = functools.partial(lax.dot_general, dimension_numbers=dims, preferred_element_type=F32)
    return dot(a_high, b_high) + (dot(a_high, b_low) + dot(a_low, b_high))


def whole(count):
    return [pl.BlockSpec(memory_space=pltpu.VMEM)] * count


def call(body, outs, args, limit=24, scratch=(), weight=0):
    return pl.pallas_call(
        body,
        out_shape=[jax.ShapeDtypeStruct(shape, F32) for shape in outs],
        in_specs=whole(len(args)),
        out_specs=whole(len(outs)),
        scratch_shapes=[pltpu.VMEM(shape, F32) for shape in scratch],
        compiler_params=pltpu.CompilerParams(vmem_limit_bytes=limit * MIB),
        cost_estimate=pl.CostEstimate(flops=weight, bytes_accessed=0, transcendentals=0) if weight else None,
    )(*args)


AXES = ("x", "z", "y", "core")
SIDE = 4


def along(axis, step, value):
    pairs = []
    for x in range(SIDE):
        for z in range(SIDE):
            for y in range(SIDE):
                for core in range(2):
                    flip = (1, 3)[step ^ core]
                    there = {"x": x, "z": z, "y": y}
                    there[axis] ^= flip
                    pairs.append((index(x, z, y, core), index(there["x"], there["z"], there["y"], core)))
    return lax.ppermute(value, AXES, pairs)


def paired(value, first):
    count = SIDE * SIDE
    pairs = []
    for low in range(first, count - 1, 2):
        pairs += [(low, low + 1), (low + 1, low)]
    return lax.ppermute(value, ("x", "z"), pairs)


def index(x, z, y, core):
    return ((x * SIDE + z) * SIDE + y) * 2 + core


def side(axis, step, core=None):
    place = lax.axis_index(axis)
    upper = place // 2
    even = lax.rem(place + upper, 2)
    core = lax.axis_index("core") if core is None else core
    return even + (upper - even) * core if step == 0 else upper + (even - upper) * core


def rows_at(which, count):
    return pl.ds(pl.multiple_of(which * count, count), count)


def sketch_ends(samples, omega):
    delays, channels, rank = omega.shape
    block = samples.shape[1]
    steps = block // LAG
    reach = delays - 1
    margin, half = reach * LAG, rank // 2
    edge = 2 * reach

    def place(at):
        inner = steps - edge
        moved = jnp.where(at < edge, at + inner, at - reach)
        return jnp.where(at < reach, at, moved)

    def body(s_hbm, o_hbm, keep_ref, send_ref, middle_ref, s_ref, high_ref, low_ref, o_ref, acc_ref, s_sem, o_sem):
        def fetch(at):
            columns = pl.ds(pl.multiple_of(place(at) * LAG, LAG), LAG)
            return pltpu.make_async_copy(s_hbm.at[:, columns], s_ref.at[:, columns], s_sem.at[at])

        def fetch_omega(d):
            return pltpu.make_async_copy(o_hbm.at[d], o_ref.at[d], o_sem.at[d])

        for d in range(delays):
            fetch_omega(d).start()
        fetch(0).start()
        acc_ref[...] = jnp.zeros_like(acc_ref)
        for d in range(delays):
            fetch_omega(d).wait()
            if d == delays - 1:
                for at in range(1, AHEAD):
                    fetch(at).start()
            high, low = split(o_ref[d].T)
            high_ref[d * rank : (d + 1) * rank, :] = high
            low_ref[d * rank : (d + 1) * rank, :] = low

        @pl.loop(0, edge)
        def _(at):
            fetch(at).wait()

            @pl.when(at + AHEAD < steps)
            def _():
                fetch(at + AHEAD).start()

            s_high, s_low = split(s_ref[:, pl.ds(pl.multiple_of(place(at) * LAG, LAG), LAG)])
            term = dot3(high_ref[...], low_ref[...], s_high, s_low, NN)
            for d in range(delays):
                to = pl.ds(pl.multiple_of((place(at) + reach - d) * LAG, LAG), LAG)
                acc_ref[:, to] += term[d * rank : (d + 1) * rank, :]

        for at in range(edge, steps):
            if at >= edge + AHEAD:
                fetch(at).start()
            fetch(at).wait()
        core = lax.axis_index("core")
        for which, ref in ((core, keep_ref), (1 - core, send_ref)):
            ref[:, :margin] = acc_ref[rows_at(which, half), :margin]
            ref[:, margin:] = acc_ref[rows_at(which, half), block:]
        middle_ref[...] = acc_ref[:, margin:block]

    ends = jax.ShapeDtypeStruct((half, 2 * margin), F32)
    return pl.pallas_call(
        body,
        out_shape=[
            ends,
            ends,
            jax.ShapeDtypeStruct((rank, block - margin), F32),
            pltpu.VMEM(samples.shape, F32),
            jax.ShapeDtypeStruct((delays * rank, channels), BF16),
            jax.ShapeDtypeStruct((delays * rank, channels), BF16),
        ],
        in_specs=[pl.BlockSpec(memory_space=pltpu.HBM)] * 2,
        out_specs=whole(6),
        scratch_shapes=[
            pltpu.VMEM(omega.shape, F32),
            pltpu.VMEM((rank, margin + block), F32),
            pltpu.SemaphoreType.DMA((steps,)),
            pltpu.SemaphoreType.DMA((delays,)),
        ],
        compiler_params=pltpu.CompilerParams(vmem_limit_bytes=20 * MIB),
        cost_estimate=pl.CostEstimate(flops=4 * WEIGHT, bytes_accessed=samples.size * 4, transcendentals=0),
    )(samples, pltpu.with_memory_space_constraint(omega, pltpu.HBM))


def sketch_middle(middle, samples, high, low, delays):
    rank, inner = middle.shape
    block = samples.shape[1]
    reach = delays - 1
    half = rank // 2

    def body(middle_ref, s_ref, high_ref, low_ref, keep_ref, send_ref, acc_ref):
        acc_ref[...] = middle_ref[...]
        for step in range(reach, block // LAG - reach):
            s_high, s_low = split(s_ref[:, step * LAG : (step + 1) * LAG])
            term = dot3(high_ref[...], low_ref[...], s_high, s_low, NN)
            for d in range(delays):
                acc_ref[:, (step - d) * LAG : (step - d + 1) * LAG] += term[d * rank : (d + 1) * rank, :]
        core = lax.axis_index("core")
        for which, ref in ((core, keep_ref), (1 - core, send_ref)):
            ref[...] = acc_ref[rows_at(which, half), :]

    return call(
        body, [(half, inner)] * 2, [middle, samples, high, low], 16, [(rank, inner)], weight=2 * WEIGHT
    )


def quarters():
    core = lax.axis_index("core")
    own, other = side("y", 0), side("y", 0, 1 - core)
    return [2 * core + own, 2 * (1 - core) + other, 2 * core + 1 - own, 2 * (1 - core) + 1 - other]


def in_order(places):
    return jnp.minimum(*places), jnp.maximum(*places)


def projection_partial(samples, sketch, delays, axis):
    channels, block = samples.shape
    quarter, width = sketch[0].shape
    count = 2 * quarter
    steps = block // WIDE
    lanes = delays * count

    def body(s_ref, mine_ref, other_ref, keep_ref, send_ref, high_ref, low_ref, acc_ref):
        core = lax.axis_index("core")
        for place, ref in ((core, mine_ref), (1 - core, other_ref)):
            high, low = split(ref[...])
            high_ref[rows_at(place, quarter), :] = high
            low_ref[rows_at(place, quarter), :] = low
        acc_ref[...] = jnp.zeros_like(acc_ref)

        @pl.loop(0, steps)
        def _(step):
            s_high, s_low = split(s_ref[:, pl.ds(pl.multiple_of(step * WIDE, WIDE), WIDE)])
            highs, lows = [], []
            for d in range(delays):
                at = pl.ds(pl.multiple_of(step * WIDE + (delays - 1 - d) * LAG, LAG), WIDE)
                highs.append(high_ref[:, at])
                lows.append(low_ref[:, at])
            acc_ref[...] += dot3(s_high, s_low, jnp.concatenate(highs, 0), jnp.concatenate(lows, 0), NT)

        which = side(axis, 0)
        for place, ref in ((which, keep_ref), (1 - which, send_ref)):
            ref[...] = acc_ref[rows_at(place, channels // 2), :]

    return pl.pallas_call(
        body,
        out_shape=[jax.ShapeDtypeStruct((channels // 2, lanes), F32)] * 2,
        in_specs=whole(3),
        out_specs=whole(2),
        scratch_shapes=[
            pltpu.VMEM((count, width), BF16),
            pltpu.VMEM((count, width), BF16),
            pltpu.VMEM((channels, lanes), F32),
        ],
        compiler_params=pltpu.CompilerParams(vmem_limit_bytes=24 * MIB),
        cost_estimate=pl.CostEstimate(flops=4 * WEIGHT, bytes_accessed=channels * block * 4, transcendentals=0),
    )(samples, *sketch)


def fold_with_gram(keep, came, axis, step, sketches, margin):
    quarter, width = sketches[0][0].shape
    rank = 4 * quarter
    count, lanes = keep.shape[0] // 2, keep.shape[1]
    tail = rank * rank // lanes

    def body(a_ref, b_ref, *refs):
        ins, outs, (sketch_ref, gram_ref) = refs[:4], refs[4:6], refs[6:]
        for place, ref in zip(quarters(), ins):
            sketch_ref[rows_at(place, quarter), :] = ref[:, margin:]
        high, low = split(sketch_ref[...])
        gram_ref[...] = dot3(high, low, high, low, NT)
        which = side(axis, step)
        for place, ref in zip((which, 1 - which), outs):
            at = rows_at(place, count)
            ref[:count, :] = a_ref[at, :] + b_ref[at, :]
            for group in range(lanes // rank):
                ref[count:, group * rank : (group + 1) * rank] = gram_ref[group * tail : (group + 1) * tail, :]

    flat = [half for pair in sketches for half in pair]
    scratch = [(rank, width - margin), (rank, rank)]
    return call(body, [(count + tail, lanes)] * 2, [keep, came, *flat], 16, scratch, weight=WEIGHT)


def fold(keep, came, axis, step):
    count = keep.shape[0] // 2

    def body(a_ref, b_ref, keep_ref, send_ref):
        which = side(axis, step)
        for place, ref in ((which, keep_ref), (1 - which, send_ref)):
            at = rows_at(place, count)
            ref[...] = a_ref[at, :] + b_ref[at, :]

    return call(body, [(count, keep.shape[1])] * 2, [keep, came], 8, weight=WEIGHT)


def add(a, b, tail=0):
    count = a.shape[0] - tail

    def body(a_ref, b_ref, out_ref, *tails):
        out_ref[...] = a_ref[:count, :] + b_ref[:count, :]
        for ref in tails:
            ref[...] = a_ref[count:, :] + b_ref[count:, :]

    return call(body, [(count, a.shape[1])] + [(tail, a.shape[1])] * (tail > 0), [a, b], 8, weight=WEIGHT)


def unfold(mine, came, axis, step):
    count = mine.shape[0]

    def body(a_ref, b_ref, out_ref):
        out_ref[rows_at(side(axis, step), count), :] = a_ref[...]
        out_ref[rows_at(1 - side(axis, step), count), :] = b_ref[...]

    return call(body, [(2 * count, mine.shape[1])], [mine, came], 8, weight=WEIGHT)[0]


def advanced(at, keep, came, one, tail):
    if at == 4:
        value = unfold(keep, came, one, 1)
        return value, value, None
    value, *rest = add(keep, came, tail if at == 3 else 0)
    return value, value, *(rest or [None])


def summed_both(first, second, sketches, margin):
    states = [first, second]
    axes = (("x", "z"), ("z", "x"))
    came = [along(axes[i][0], 0, states[i][1]) for i in range(2)]
    for at in range(5):
        for i in range(2):
            arrived, _ = lax.optimization_barrier((came[i], states[1 - i][1]))
            one, two = axes[i]
            if at > 0:
                tail = 0 if i else states[i][0].shape[0] - first[0].shape[0] // 2
                *states[i], rest = advanced(at, states[i][0], arrived, one, tail)
                if rest is not None:
                    gram = add(rest, along(one, 0, rest))[0]
            elif i == 0:
                states[i] = fold_with_gram(states[i][0], arrived, one, 1, sketches, margin)
            else:
                states[i] = fold(states[i][0], arrived, one, 1)
            came[i] = along(*((one, 1), (two, 0), (two, 1), (one, 1), (one, 0))[at], states[i][1])
    return (states[0][0], came[0]), (states[1][0], came[1]), gram


def inverse_factor(tail, rank):
    deep, delays = tail.shape[0], tail.shape[1] // rank
    panel = 16

    def body(tail_ref, out_ref, left_ref, right_ref):
        for d in range(delays):
            left_ref[d * deep : (d + 1) * deep, :] = tail_ref[:, d * rank : (d + 1) * rank]
        square = (rank, rank)
        same = lax.broadcasted_iota(jnp.int32, square, 0) == lax.broadcasted_iota(jnp.int32, square, 1)
        right_ref[...] = jnp.where(same, 1.0, 0.0)
        row = lax.broadcasted_iota(jnp.int32, (panel, rank), 0)
        for top in range(0, rank, panel):
            end = top + panel
            left, right = left_ref[top:end, :], right_ref[top:end, :]
            columns = [jnp.broadcast_to(left[:, top + m : top + m + 1], (panel, rank)) for m in range(panel)]
            pivots = jnp.zeros((panel, rank), F32)
            for j in range(panel):
                reciprocal = 1.0 / columns[j][j : j + 1, :]
                pivots = jnp.where(row == j, reciprocal, pivots)
                factor = jnp.where(row > j, columns[j] * reciprocal, 0.0)
                for m in range(j + 1, panel):
                    columns[m] = columns[m] - factor * columns[m][j : j + 1, :]
                left = left - factor * left[j : j + 1, :]
                right = right - factor * right[j : j + 1, :]
            if end < rank:
                factors = (left * pivots).T
                below_left, below_right = left_ref[end:, :], right_ref[end:, :]
                for j in range(panel):
                    factor = factors[end:, j : j + 1]
                    below_left = below_left - factor * left[j : j + 1, :]
                    below_right = below_right - factor * right[j : j + 1, :]
                left_ref[end:, :] = below_left
                right_ref[end:, :] = below_right
            out_ref[top:end, :] = right * lax.sqrt(pivots)

    return pl.pallas_call(
        body,
        out_shape=jax.ShapeDtypeStruct((rank, rank), F32),
        in_specs=whole(1),
        out_specs=whole(1)[0],
        scratch_shapes=[pltpu.VMEM((rank, rank), F32)] * 2,
        compiler_params=pltpu.CompilerParams(vmem_limit_bytes=8 * MIB),
    )(tail)


def shards(samples, omega):
    delays, channels, rank = omega.shape
    block = samples.shape[1]
    margin = (delays - 1) * LAG
    inner = block - margin
    width = margin + block
    half, quarter = rank // 2, rank // 4
    total = block * SIDE * SIDE

    ends, ends_send, middle, samples, high, low = sketch_ends(samples, omega)
    middle, middle_send = sketch_middle(middle, samples, high, low, delays)
    ends, ends_send = fold(ends, lax.ppermute(ends_send, "core", [(0, 1), (1, 0)]), "y", 0)
    middle, middle_send = fold(middle, lax.ppermute(middle_send, "core", [(0, 1), (1, 0)]), "y", 0)
    ends_came = along("y", 0, ends_send)
    middle_came = along("y", 0, middle_send)
    (ends,) = add(ends, ends_came)
    ends_came = along("y", 1, ends)
    (middle,) = add(middle, middle_came)
    middle_came = along("y", 1, middle)

    def even():
        return lax.rem(lax.axis_index("z"), 2) == 0

    def add_ends(a_ref, b_ref, left_ref, right_ref, one_ref, two_ref):
        left_ref[...] = a_ref[:, :margin] + b_ref[:, :margin]
        right_ref[...] = a_ref[:, margin:] + b_ref[:, margin:]
        one_ref[...] = jnp.where(even(), right_ref[...], left_ref[...])
        two_ref[...] = jnp.where(even(), left_ref[...], right_ref[...])

    left, right, one, two = call(add_ends, [(quarter, margin)] * 4, [ends, ends_came], 8)
    one, two = paired(one, 0), paired(two, 1)

    def join(left_ref, right_ref, one_ref, two_ref, middle_ref, middle_came_ref, out_ref):
        inside = lax.axis_index("x") + lax.axis_index("z") > 0
        left_came = jnp.where(even(), two_ref[...], one_ref[...])
        right_came = jnp.where(even(), one_ref[...], two_ref[...])
        out_ref[:, :margin] = jnp.where(inside, left_ref[...] + left_came, 0.0)
        out_ref[:, margin:block] = middle_ref[...] + middle_came_ref[...]
        out_ref[:, block:] = right_ref[...] + right_came

    (mine,) = call(join, [(quarter, width)], [left, right, one, two, middle, middle_came], 8)
    sketches = [(mine, lax.ppermute(mine, "core", [(0, 1), (1, 0)]))]
    mine = along("y", 0, mine)

    first = projection_partial(samples, sketches[0], delays, "x")
    mine, *first = lax.optimization_barrier((mine, *first))
    sketches.append((mine, lax.ppermute(mine, "core", [(0, 1), (1, 0)])))
    second = projection_partial(samples, sketches[1], delays, "z")
    first, second, gram = summed_both(first, second, sketches, margin)
    inverse = inverse_factor(gram, rank)

    def multiplied(turned_ref, part, ref, put):
        pick = [turned_ref[rows_at(q, quarter), :] for q in in_order(quarters()[2 * part : 2 * part + 2])]
        none = [jnp.zeros((half, rank), F32)]
        pick = [split(jnp.concatenate(m, 0)) for m in (pick + none, none + pick)]
        for pair in range(delays // 2):
            a_high, a_low = split(ref[:, pair * rank : (pair + 1) * rank])
            for odd in range(2):
                put(2 * pair + odd, dot3(a_high, a_low, *pick[odd], NN))

    def finish_first(inverse_ref, *refs):
        rows, ins, outs, (mine_ref, sketch_ref, sem, both_ref) = refs[:4], refs[4:7], refs[7:11], refs[11:]
        basis_ref, out_ref, partial_ref, turned_ref = outs
        turned_ref[...] = inverse_ref[...].T
        which = side("z", 0)
        here = side("x", 0)

        def put_first(place):
            def put(d, value):
                both_ref[d, rows_at(place, channels // 2), :] = value

            return put

        multiplied(turned_ref, 0, ins[0], put_first(here))
        multiplied(turned_ref, 0, ins[1], put_first(1 - here))

        def copy(d):
            return pltpu.make_async_copy(mine_ref.at[d], out_ref.at[d, rows_at(which, channels // 2), :], sem.at[d])

        def put_second(d, value):
            mine_ref[d] = both_ref[d, rows_at(which, channels // 2), :] + value
            copy(d).start()

        multiplied(turned_ref, 1, ins[2], put_second)
        for d in range(delays):
            partial_ref[d] = both_ref[d, rows_at(1 - which, channels // 2), :]
        core, y = lax.axis_index("core"), lax.axis_index("y")
        columns = block // 8
        at = pl.ds(pl.multiple_of(margin + (y * 2 + core) * columns, columns), columns)
        for place, ref in zip(quarters(), rows):
            sketch_ref[rows_at(place, quarter), :] = ref[:, at]
        high, low = split(inverse_ref[...])
        s_high, s_low = split(sketch_ref[...])
        basis_ref[...] = math.sqrt(total) * dot3(high, low, s_high, s_low, NN)
        for d in range(delays):
            copy(d).wait()

    shape, part_shape = (delays, channels, rank), (delays, channels // 2, rank)
    outs = [jax.ShapeDtypeStruct(s, F32) for s in ((rank, block // 8), shape, part_shape, (rank, rank))]
    basis, projection, partial, turned = pl.pallas_call(
        finish_first,
        out_shape=outs,
        in_specs=whole(8),
        out_specs=whole(1) + [pl.BlockSpec(memory_space=pltpu.HBM)] + whole(2),
        scratch_shapes=[
            pltpu.VMEM(part_shape, F32),
            pltpu.VMEM((rank, block // 8), F32),
            pltpu.SemaphoreType.DMA((delays,)),
            pltpu.VMEM(shape, F32),
        ],
        compiler_params=pltpu.CompilerParams(vmem_limit_bytes=24 * MIB),
    )(inverse, *sketches[0], *sketches[1], *first, second[0])

    def finish_second(turned_ref, partial_ref, came_ref, _, out_ref, mine_ref, sem):
        which = 1 - side("z", 0)

        def copy(d):
            return pltpu.make_async_copy(mine_ref.at[d], out_ref.at[d, rows_at(which, channels // 2), :], sem.at[d])

        def put(d, value):
            mine_ref[d] = partial_ref[d] + value
            copy(d).start()

        multiplied(turned_ref, 1, came_ref, put)
        for d in range(delays):
            copy(d).wait()

    projection = pl.pallas_call(
        finish_second,
        out_shape=outs[1],
        in_specs=whole(3) + [pl.BlockSpec(memory_space=pltpu.HBM)],
        out_specs=pl.BlockSpec(memory_space=pltpu.HBM),
        scratch_shapes=[pltpu.VMEM(part_shape, F32), pltpu.SemaphoreType.DMA((delays,))],
        input_output_aliases={3: 0},
        compiler_params=pltpu.CompilerParams(vmem_limit_bytes=16 * MIB),
    )(turned, partial, second[1], projection)
    return basis, projection


def solution(mesh):
    fine = Mesh(mesh.devices.reshape(SIDE, SIDE, SIDE, 2), AXES)
    tm, chan = ("x", "z"), ("y", "core")
    return jax.shard_map(
        shards,
        mesh=fine,
        in_specs=(P(chan, tm), P(None, chan, None)),
        out_specs=(P(None, tm + chan), P(None, chan, None)),
        check_vma=False,
    )
```

```python
import functools
import math

import jax
import jax.numpy as jnp
from jax import lax
from jax.experimental import pallas as pl
from jax.experimental.pallas import tpu as pltpu
from jax.sharding import Mesh
from jax.sharding import PartitionSpec as P

LAG = 512
WIDE = 1024
AHEAD = 3
F32 = jnp.float32
BF16 = jnp.bfloat16
NT = (((1,), (1,)), ((), ()))
NN = (((1,), (0,)), ((), ()))
MIB = 1024 * 1024
WEIGHT = int(2e10)


def split(value):
    high = value.astype(BF16)
    return high, (value - high.astype(F32)).astype(BF16)


def dot3(a_high, a_low, b_high, b_low, dims):
    dot = functools.partial(lax.dot_general, dimension_numbers=dims, preferred_element_type=F32)
    return dot(a_high, b_high) + (dot(a_high, b_low) + dot(a_low, b_high))


def whole(count):
    return [pl.BlockSpec(memory_space=pltpu.VMEM)] * count


def call(body, outs, args, limit=24, scratch=(), weight=0):
    return pl.pallas_call(
        body,
        out_shape=[jax.ShapeDtypeStruct(shape, F32) for shape in outs],
        in_specs=whole(len(args)),
        out_specs=whole(len(outs)),
        scratch_shapes=[pltpu.VMEM(shape, F32) for shape in scratch],
        compiler_params=pltpu.CompilerParams(vmem_limit_bytes=limit * MIB),
        cost_estimate=pl.CostEstimate(flops=weight, bytes_accessed=0, transcendentals=0) if weight else None,
    )(*args)


AXES = ("x", "z", "y", "core")
SIDE = 4


def along(axis, step, value):
    pairs = []
    for x in range(SIDE):
        for z in range(SIDE):
            for y in range(SIDE):
                for core in range(2):
                    flip = (1, 3)[step ^ core]
                    there = {"x": x, "z": z, "y": y}
                    there[axis] ^= flip
                    pairs.append((index(x, z, y, core), index(there["x"], there["z"], there["y"], core)))
    return lax.ppermute(value, AXES, pairs)


def paired(value, first):
    count = SIDE * SIDE
    pairs = []
    for low in range(first, count - 1, 2):
        pairs += [(low, low + 1), (low + 1, low)]
    return lax.ppermute(value, ("x", "z"), pairs)


def index(x, z, y, core):
    return ((x * SIDE + z) * SIDE + y) * 2 + core


def side(axis, step, core=None):
    place = lax.axis_index(axis)
    upper = place // 2
    even = lax.rem(place + upper, 2)
    core = lax.axis_index("core") if core is None else core
    return even + (upper - even) * core if step == 0 else upper + (even - upper) * core


def rows_at(which, count):
    return pl.ds(pl.multiple_of(which * count, count), count)


def sketch_ends(samples, omega):
    delays, channels, rank = omega.shape
    block = samples.shape[1]
    steps = block // LAG
    reach = delays - 1
    margin, half = reach * LAG, rank // 2
    edge = 2 * reach

    def place(at):
        inner = steps - edge
        moved = jnp.where(at < edge, at + inner, at - reach)
        return jnp.where(at < reach, at, moved)

    def body(s_hbm, o_hbm, keep_ref, send_ref, middle_ref, s_ref, high_ref, low_ref, o_ref, acc_ref, s_sem, o_sem):
        def fetch(at):
            columns = pl.ds(pl.multiple_of(place(at) * LAG, LAG), LAG)
            return pltpu.make_async_copy(s_hbm.at[:, columns], s_ref.at[:, columns], s_sem.at[at])

        def fetch_omega(d):
            return pltpu.make_async_copy(o_hbm.at[d], o_ref.at[d], o_sem.at[d])

        for d in range(delays):
            fetch_omega(d).start()
        fetch(0).start()
        acc_ref[...] = jnp.zeros_like(acc_ref)
        for d in range(delays):
            fetch_omega(d).wait()
            if d == delays - 1:
                for at in range(1, AHEAD):
                    fetch(at).start()
            high, low = split(o_ref[d].T)
            high_ref[d * rank : (d + 1) * rank, :] = high
            low_ref[d * rank : (d + 1) * rank, :] = low

        @pl.loop(0, edge)
        def _(at):
            fetch(at).wait()

            @pl.when(at + AHEAD < steps)
            def _():
                fetch(at + AHEAD).start()

            s_high, s_low = split(s_ref[:, pl.ds(pl.multiple_of(place(at) * LAG, LAG), LAG)])
            term = dot3(high_ref[...], low_ref[...], s_high, s_low, NN)
            for d in range(delays):
                to = pl.ds(pl.multiple_of((place(at) + reach - d) * LAG, LAG), LAG)
                acc_ref[:, to] += term[d * rank : (d + 1) * rank, :]

        for at in range(edge, steps):
            if at >= edge + AHEAD:
                fetch(at).start()
            fetch(at).wait()
        core = lax.axis_index("core")
        for which, ref in ((core, keep_ref), (1 - core, send_ref)):
            ref[:, :margin] = acc_ref[rows_at(which, half), :margin]
            ref[:, margin:] = acc_ref[rows_at(which, half), block:]
        middle_ref[...] = acc_ref[:, margin:block]

    ends = jax.ShapeDtypeStruct((half, 2 * margin), F32)
    return pl.pallas_call(
        body,
        out_shape=[
            ends,
            ends,
            jax.ShapeDtypeStruct((rank, block - margin), F32),
            pltpu.VMEM(samples.shape, F32),
            jax.ShapeDtypeStruct((delays * rank, channels), BF16),
            jax.ShapeDtypeStruct((delays * rank, channels), BF16),
        ],
        in_specs=[pl.BlockSpec(memory_space=pltpu.HBM)] * 2,
        out_specs=whole(6),
        scratch_shapes=[
            pltpu.VMEM(omega.shape, F32),
            pltpu.VMEM((rank, margin + block), F32),
            pltpu.SemaphoreType.DMA((steps,)),
            pltpu.SemaphoreType.DMA((delays,)),
        ],
        compiler_params=pltpu.CompilerParams(vmem_limit_bytes=20 * MIB),
        cost_estimate=pl.CostEstimate(flops=4 * WEIGHT, bytes_accessed=samples.size * 4, transcendentals=0),
    )(samples, pltpu.with_memory_space_constraint(omega, pltpu.HBM))


def sketch_middle(middle, samples, high, low, delays):
    rank, inner = middle.shape
    block = samples.shape[1]
    reach = delays - 1
    half = rank // 2

    def body(middle_ref, s_ref, high_ref, low_ref, keep_ref, send_ref, acc_ref):
        acc_ref[...] = middle_ref[...]
        for step in range(reach, block // LAG - reach):
            s_high, s_low = split(s_ref[:, step * LAG : (step + 1) * LAG])
            term = dot3(high_ref[...], low_ref[...], s_high, s_low, NN)
            for d in range(delays):
                acc_ref[:, (step - d) * LAG : (step - d + 1) * LAG] += term[d * rank : (d + 1) * rank, :]
        core = lax.axis_index("core")
        for which, ref in ((core, keep_ref), (1 - core, send_ref)):
            ref[...] = acc_ref[rows_at(which, half), :]

    return call(
        body, [(half, inner)] * 2, [middle, samples, high, low], 16, [(rank, inner)], weight=2 * WEIGHT
    )


def quarters():
    core = lax.axis_index("core")
    own, other = side("y", 0), side("y", 0, 1 - core)
    return [2 * core + own, 2 * (1 - core) + other, 2 * core + 1 - own, 2 * (1 - core) + 1 - other]


def in_order(places):
    return jnp.minimum(*places), jnp.maximum(*places)


def projection_partial(samples, sketch, delays):
    channels, block = samples.shape
    quarter, width = sketch[0].shape
    count = 2 * quarter
    steps = block // WIDE
    lanes = delays * count

    def body(s_ref, mine_ref, other_ref, keep_ref, send_ref, high_ref, low_ref, acc_ref):
        core = lax.axis_index("core")
        for place, ref in ((core, mine_ref), (1 - core, other_ref)):
            high, low = split(ref[...])
            high_ref[rows_at(place, quarter), :] = high
            low_ref[rows_at(place, quarter), :] = low
        acc_ref[...] = jnp.zeros_like(acc_ref)

        @pl.loop(0, steps)
        def _(step):
            s_high, s_low = split(s_ref[:, pl.ds(pl.multiple_of(step * WIDE, WIDE), WIDE)])
            highs, lows = [], []
            for d in range(delays):
                at = pl.ds(pl.multiple_of(step * WIDE + (delays - 1 - d) * LAG, LAG), WIDE)
                highs.append(high_ref[:, at])
                lows.append(low_ref[:, at])
            acc_ref[...] += dot3(s_high, s_low, jnp.concatenate(highs, 0), jnp.concatenate(lows, 0), NT)

        which = side(*ROUTE[0])
        for place, ref in ((which, keep_ref), (1 - which, send_ref)):
            ref[...] = acc_ref[rows_at(place, channels // 2), :]

    return pl.pallas_call(
        body,
        out_shape=[jax.ShapeDtypeStruct((channels // 2, lanes), F32)] * 2,
        in_specs=whole(3),
        out_specs=whole(2),
        scratch_shapes=[
            pltpu.VMEM((count, width), BF16),
            pltpu.VMEM((count, width), BF16),
            pltpu.VMEM((channels, lanes), F32),
        ],
        compiler_params=pltpu.CompilerParams(vmem_limit_bytes=24 * MIB),
        cost_estimate=pl.CostEstimate(flops=4 * WEIGHT, bytes_accessed=channels * block * 4, transcendentals=0),
    )(samples, *sketch)


def fold_with_gram(keep, came, axis, step, sketches, margin):
    quarter, width = sketches[0][0].shape
    rank = 4 * quarter
    count, lanes = keep.shape[0] // 2, keep.shape[1]
    tail = rank * rank // lanes

    def body(a_ref, b_ref, *refs):
        ins, outs, (sketch_ref, gram_ref) = refs[:4], refs[4:6], refs[6:]
        for place, ref in zip(quarters(), ins):
            sketch_ref[rows_at(place, quarter), :] = ref[:, margin:]
        high, low = split(sketch_ref[...])
        gram_ref[...] = dot3(high, low, high, low, NT)
        which = side(axis, step)
        for place, ref in zip((which, 1 - which), outs):
            at = rows_at(place, count)
            ref[:count, :] = a_ref[at, :] + b_ref[at, :]
            for group in range(lanes // rank):
                ref[count:, group * rank : (group + 1) * rank] = gram_ref[group * tail : (group + 1) * tail, :]

    flat = [half for pair in sketches for half in pair]
    scratch = [(rank, width - margin), (rank, rank)]
    return call(body, [(count + tail, lanes)] * 2, [keep, came, *flat], 16, scratch, weight=WEIGHT)


def fold(keep, came, axis, step):
    count = keep.shape[0] // 2

    def body(a_ref, b_ref, keep_ref, send_ref):
        which = side(axis, step)
        for place, ref in ((which, keep_ref), (1 - which, send_ref)):
            at = rows_at(place, count)
            ref[...] = a_ref[at, :] + b_ref[at, :]

    return call(body, [(count, keep.shape[1])] * 2, [keep, came], 8, weight=WEIGHT)


def add(a, b, tail=0):
    count = a.shape[0] - tail

    def body(a_ref, b_ref, out_ref, *tails):
        out_ref[...] = a_ref[:count, :] + b_ref[:count, :]
        for ref in tails:
            ref[...] = a_ref[count:, :] + b_ref[count:, :]

    return call(body, [(count, a.shape[1])] + [(tail, a.shape[1])] * (tail > 0), [a, b], 8, weight=WEIGHT)


def unfold(mine, came, axis, step):
    count = mine.shape[0]

    def body(a_ref, b_ref, out_ref):
        out_ref[rows_at(side(axis, step), count), :] = a_ref[...]
        out_ref[rows_at(1 - side(axis, step), count), :] = b_ref[...]

    return call(body, [(2 * count, mine.shape[1])], [mine, came], 8, weight=WEIGHT)[0]


ROUTE = (("z", 0), ("x", 0), ("x", 1), ("z", 1), ("x", 0), ("z", 0))


def advanced(at, keep, came, tail):
    if at == 4:
        value = unfold(keep, came, *ROUTE[at])
        return value, value, None
    value, *rest = add(keep, came, tail if at == 3 else 0)
    return value, value, *(rest or [None])


def summed_both(first, second, sketches, margin):
    states = [first, second]
    came = [along(*ROUTE[0], state[1]) for state in states]
    for at in range(5):
        for i in range(2):
            arrived, _ = lax.optimization_barrier((came[i], states[1 - i][1]))
            if at > 0:
                tail = 0 if i else states[i][0].shape[0] - first[0].shape[0] // 2
                *states[i], rest = advanced(at, states[i][0], arrived, tail)
                if rest is not None:
                    gram = add(rest, along(*ROUTE[0], rest))[0]
            elif i == 0:
                states[i] = fold_with_gram(states[i][0], arrived, *ROUTE[1], sketches, margin)
            else:
                states[i] = fold(states[i][0], arrived, *ROUTE[1])
            came[i] = along(*ROUTE[at + 1], states[i][1])
    return (states[0][0], came[0]), (states[1][0], came[1]), gram


def inverse_factor(tail, rank):
    deep, delays = tail.shape[0], tail.shape[1] // rank
    panel = 16

    def body(tail_ref, out_ref, left_ref, right_ref):
        for d in range(delays):
            left_ref[d * deep : (d + 1) * deep, :] = tail_ref[:, d * rank : (d + 1) * rank]
        square = (rank, rank)
        same = lax.broadcasted_iota(jnp.int32, square, 0) == lax.broadcasted_iota(jnp.int32, square, 1)
        right_ref[...] = jnp.where(same, 1.0, 0.0)
        row = lax.broadcasted_iota(jnp.int32, (panel, rank), 0)
        for top in range(0, rank, panel):
            end = top + panel
            left, right = left_ref[top:end, :], right_ref[top:end, :]
            columns = [jnp.broadcast_to(left[:, top + m : top + m + 1], (panel, rank)) for m in range(panel)]
            pivots = jnp.zeros((panel, rank), F32)
            for j in range(panel):
                reciprocal = 1.0 / columns[j][j : j + 1, :]
                pivots = jnp.where(row == j, reciprocal, pivots)
                factor = jnp.where(row > j, columns[j] * reciprocal, 0.0)
                for m in range(j + 1, panel):
                    columns[m] = columns[m] - factor * columns[m][j : j + 1, :]
                left = left - factor * left[j : j + 1, :]
                right = right - factor * right[j : j + 1, :]
            if end < rank:
                factors = (left * pivots).T
                below_left, below_right = left_ref[end:, :], right_ref[end:, :]
                for j in range(panel):
                    factor = factors[end:, j : j + 1]
                    below_left = below_left - factor * left[j : j + 1, :]
                    below_right = below_right - factor * right[j : j + 1, :]
                left_ref[end:, :] = below_left
                right_ref[end:, :] = below_right
            out_ref[top:end, :] = right * lax.sqrt(pivots)

    return pl.pallas_call(
        body,
        out_shape=jax.ShapeDtypeStruct((rank, rank), F32),
        in_specs=whole(1),
        out_specs=whole(1)[0],
        scratch_shapes=[pltpu.VMEM((rank, rank), F32)] * 2,
        compiler_params=pltpu.CompilerParams(vmem_limit_bytes=8 * MIB),
    )(tail)


def shards(samples, omega):
    delays, channels, rank = omega.shape
    block = samples.shape[1]
    margin = (delays - 1) * LAG
    inner = block - margin
    width = margin + block
    half, quarter = rank // 2, rank // 4
    total = block * SIDE * SIDE

    ends, ends_send, middle, samples, high, low = sketch_ends(samples, omega)
    middle, middle_send = sketch_middle(middle, samples, high, low, delays)
    ends, ends_send = fold(ends, lax.ppermute(ends_send, "core", [(0, 1), (1, 0)]), "y", 0)
    middle, middle_send = fold(middle, lax.ppermute(middle_send, "core", [(0, 1), (1, 0)]), "y", 0)
    ends_came = along("y", 0, ends_send)
    middle_came = along("y", 0, middle_send)
    (ends,) = add(ends, ends_came)
    ends_came = along("y", 1, ends)
    (middle,) = add(middle, middle_came)
    middle_came = along("y", 1, middle)

    def even():
        return lax.rem(lax.axis_index("z"), 2) == 0

    def add_ends(a_ref, b_ref, left_ref, right_ref, one_ref, two_ref):
        left_ref[...] = a_ref[:, :margin] + b_ref[:, :margin]
        right_ref[...] = a_ref[:, margin:] + b_ref[:, margin:]
        one_ref[...] = jnp.where(even(), right_ref[...], left_ref[...])
        two_ref[...] = jnp.where(even(), left_ref[...], right_ref[...])

    left, right, one, two = call(add_ends, [(quarter, margin)] * 4, [ends, ends_came], 8)
    one, two = paired(one, 0), paired(two, 1)

    def join(left_ref, right_ref, one_ref, two_ref, middle_ref, middle_came_ref, out_ref):
        inside = lax.axis_index("x") + lax.axis_index("z") > 0
        left_came = jnp.where(even(), two_ref[...], one_ref[...])
        right_came = jnp.where(even(), one_ref[...], two_ref[...])
        out_ref[:, :margin] = jnp.where(inside, left_ref[...] + left_came, 0.0)
        out_ref[:, margin:block] = middle_ref[...] + middle_came_ref[...]
        out_ref[:, block:] = right_ref[...] + right_came

    (mine,) = call(join, [(quarter, width)], [left, right, one, two, middle, middle_came], 8)
    sketches = [(mine, lax.ppermute(mine, "core", [(0, 1), (1, 0)]))]
    mine = along("y", 0, mine)

    first = projection_partial(samples, sketches[0], delays)
    mine, *first = lax.optimization_barrier((mine, *first))
    sketches.append((mine, lax.ppermute(mine, "core", [(0, 1), (1, 0)])))
    second = projection_partial(samples, sketches[1], delays)
    first, second, gram = summed_both(first, second, sketches, margin)
    inverse = inverse_factor(gram, rank)

    def multiplied(turned_ref, part, ref, put):
        pick = [turned_ref[rows_at(q, quarter), :] for q in in_order(quarters()[2 * part : 2 * part + 2])]
        none = [jnp.zeros((half, rank), F32)]
        pick = [split(jnp.concatenate(m, 0)) for m in (pick + none, none + pick)]
        for pair in range(delays // 2):
            a_high, a_low = split(ref[:, pair * rank : (pair + 1) * rank])
            for odd in range(2):
                put(2 * pair + odd, dot3(a_high, a_low, *pick[odd], NN))

    def finish_first(inverse_ref, *refs):
        rows, ins, outs, (mine_ref, sketch_ref, sem, both_ref) = refs[:4], refs[4:7], refs[7:11], refs[11:]
        basis_ref, out_ref, partial_ref, turned_ref = outs
        turned_ref[...] = inverse_ref[...].T
        which = side(*ROUTE[0])

        def put_first(place):
            def put(d, value):
                both_ref[d, rows_at(place, channels // 2), :] = value

            return put

        multiplied(turned_ref, 0, ins[0], put_first(which))
        multiplied(turned_ref, 0, ins[1], put_first(1 - which))

        def copy(d):
            return pltpu.make_async_copy(mine_ref.at[d], out_ref.at[d, rows_at(which, channels // 2), :], sem.at[d])

        def put_second(d, value):
            mine_ref[d] = both_ref[d, rows_at(which, channels // 2), :] + value
            copy(d).start()

        multiplied(turned_ref, 1, ins[2], put_second)
        for d in range(delays):
            partial_ref[d] = both_ref[d, rows_at(1 - which, channels // 2), :]
        core, y = lax.axis_index("core"), lax.axis_index("y")
        columns = block // 8
        at = pl.ds(pl.multiple_of(margin + (y * 2 + core) * columns, columns), columns)
        for place, ref in zip(quarters(), rows):
            sketch_ref[rows_at(place, quarter), :] = ref[:, at]
        high, low = split(inverse_ref[...])
        s_high, s_low = split(sketch_ref[...])
        basis_ref[...] = math.sqrt(total) * dot3(high, low, s_high, s_low, NN)
        for d in range(delays):
            copy(d).wait()

    shape, part_shape = (delays, channels, rank), (delays, channels // 2, rank)
    outs = [jax.ShapeDtypeStruct(s, F32) for s in ((rank, block // 8), shape, part_shape, (rank, rank))]
    basis, projection, partial, turned = pl.pallas_call(
        finish_first,
        out_shape=outs,
        in_specs=whole(8),
        out_specs=whole(1) + [pl.BlockSpec(memory_space=pltpu.HBM)] + whole(2),
        scratch_shapes=[
            pltpu.VMEM(part_shape, F32),
            pltpu.VMEM((rank, block // 8), F32),
            pltpu.SemaphoreType.DMA((delays,)),
            pltpu.VMEM(shape, F32),
        ],
        compiler_params=pltpu.CompilerParams(vmem_limit_bytes=24 * MIB),
    )(inverse, *sketches[0], *sketches[1], *first, second[0])

    def finish_second(turned_ref, partial_ref, came_ref, _, out_ref, mine_ref, sem):
        which = 1 - side(*ROUTE[0])

        def copy(d):
            return pltpu.make_async_copy(mine_ref.at[d], out_ref.at[d, rows_at(which, channels // 2), :], sem.at[d])

        def put(d, value):
            mine_ref[d] = partial_ref[d] + value
            copy(d).start()

        multiplied(turned_ref, 1, came_ref, put)
        for d in range(delays):
            copy(d).wait()

    projection = pl.pallas_call(
        finish_second,
        out_shape=outs[1],
        in_specs=whole(3) + [pl.BlockSpec(memory_space=pltpu.HBM)],
        out_specs=pl.BlockSpec(memory_space=pltpu.HBM),
        scratch_shapes=[pltpu.VMEM(part_shape, F32), pltpu.SemaphoreType.DMA((delays,))],
        input_output_aliases={3: 0},
        compiler_params=pltpu.CompilerParams(vmem_limit_bytes=16 * MIB),
    )(turned, partial, second[1], projection)
    return basis, projection


def solution(mesh):
    fine = Mesh(mesh.devices.reshape(SIDE, SIDE, SIDE, 2), AXES)
    tm, chan = ("x", "z"), ("y", "core")
    return jax.shard_map(
        shards,
        mesh=fine,
        in_specs=(P(chan, tm), P(None, chan, None)),
        out_specs=(P(None, tm + chan), P(None, chan, None)),
        check_vma=False,
    )
```

```python
import functools
import math

import jax
import jax.numpy as jnp
from jax import lax
from jax.experimental import pallas as pl
from jax.experimental.pallas import tpu as pltpu
from jax.sharding import Mesh
from jax.sharding import PartitionSpec as P

LAG = 512
WIDE = 2048
AHEAD = 4
F32 = jnp.float32
BF16 = jnp.bfloat16
NT = (((1,), (1,)), ((), ()))
NN = (((1,), (0,)), ((), ()))
MIB = 1024 * 1024
WEIGHT = int(2e10)


def split(value):
    high = value.astype(BF16)
    return high, (value - high.astype(F32)).astype(BF16)


def dot3(a_high, a_low, b_high, b_low, dims):
    dot = functools.partial(lax.dot_general, dimension_numbers=dims, preferred_element_type=F32)
    return dot(a_high, b_high) + (dot(a_high, b_low) + dot(a_low, b_high))


def whole(count):
    return [pl.BlockSpec(memory_space=pltpu.VMEM)] * count


def call(body, outs, args, limit=24, scratch=(), weight=0):
    return pl.pallas_call(
        body,
        out_shape=[jax.ShapeDtypeStruct(shape, F32) for shape in outs],
        in_specs=whole(len(args)),
        out_specs=whole(len(outs)),
        scratch_shapes=[pltpu.VMEM(shape, F32) for shape in scratch],
        compiler_params=pltpu.CompilerParams(vmem_limit_bytes=limit * MIB),
        cost_estimate=pl.CostEstimate(flops=weight, bytes_accessed=0, transcendentals=0) if weight else None,
    )(*args)


AXES = ("x", "z", "y", "core")
SIDE = 4


def along(axis, step, value):
    pairs = []
    for x in range(SIDE):
        for z in range(SIDE):
            for y in range(SIDE):
                for core in range(2):
                    flip = (1, 3)[step ^ core]
                    there = {"x": x, "z": z, "y": y}
                    there[axis] ^= flip
                    pairs.append((index(x, z, y, core), index(there["x"], there["z"], there["y"], core)))
    return lax.ppermute(value, AXES, pairs)


def paired(value, first):
    count = SIDE * SIDE
    pairs = []
    for low in range(first, count - 1, 2):
        pairs += [(low, low + 1), (low + 1, low)]
    return lax.ppermute(value, ("x", "z"), pairs)


def index(x, z, y, core):
    return ((x * SIDE + z) * SIDE + y) * 2 + core


def side(axis, step, core=None):
    place = lax.axis_index(axis)
    upper = place // 2
    even = lax.rem(place + upper, 2)
    core = lax.axis_index("core") if core is None else core
    return even + (upper - even) * core if step == 0 else upper + (even - upper) * core


def rows_at(which, count):
    return pl.ds(pl.multiple_of(which * count, count), count)


def sketch_ends(samples, omega):
    delays, channels, rank = omega.shape
    block = samples.shape[1]
    steps = block // LAG
    reach = delays - 1
    margin, half = reach * LAG, rank // 2
    edge = 2 * reach

    def place(at):
        inner = steps - edge
        moved = jnp.where(at < edge, at + inner, at - reach)
        return jnp.where(at < reach, at, moved)

    def body(s_hbm, o_hbm, keep_ref, send_ref, middle_ref, s_ref, high_ref, low_ref, o_ref, acc_ref, s_sem, o_sem):
        def fetch(at):
            columns = pl.ds(pl.multiple_of(place(at) * LAG, LAG), LAG)
            return pltpu.make_async_copy(s_hbm.at[:, columns], s_ref.at[:, columns], s_sem.at[at])

        def fetch_omega(d):
            return pltpu.make_async_copy(o_hbm.at[d], o_ref.at[d], o_sem.at[d])

        for d in range(delays):
            fetch_omega(d).start()
        fetch(0).start()
        acc_ref[...] = jnp.zeros_like(acc_ref)
        for d in range(delays):
            fetch_omega(d).wait()
            if d == delays - 1:
                for at in range(1, AHEAD):
                    fetch(at).start()
            high, low = split(o_ref[d].T)
            high_ref[d * rank : (d + 1) * rank, :] = high
            low_ref[d * rank : (d + 1) * rank, :] = low

        @pl.loop(0, edge)
        def _(at):
            fetch(at).wait()

            @pl.when(at + AHEAD < steps)
            def _():
                fetch(at + AHEAD).start()

            s_high, s_low = split(s_ref[:, pl.ds(pl.multiple_of(place(at) * LAG, LAG), LAG)])
            term = dot3(high_ref[...], low_ref[...], s_high, s_low, NN)
            for d in range(delays):
                to = pl.ds(pl.multiple_of((place(at) + reach - d) * LAG, LAG), LAG)
                acc_ref[:, to] += term[d * rank : (d + 1) * rank, :]

        for at in range(edge, steps):
            if at >= edge + AHEAD:
                fetch(at).start()
            fetch(at).wait()
        core = lax.axis_index("core")
        for which, ref in ((core, keep_ref), (1 - core, send_ref)):
            ref[:, :margin] = acc_ref[rows_at(which, half), :margin]
            ref[:, margin:] = acc_ref[rows_at(which, half), block:]
        middle_ref[...] = acc_ref[:, margin:block]

    ends = jax.ShapeDtypeStruct((half, 2 * margin), F32)
    return pl.pallas_call(
        body,
        out_shape=[
            ends,
            ends,
            jax.ShapeDtypeStruct((rank, block - margin), F32),
            pltpu.VMEM(samples.shape, F32),
            jax.ShapeDtypeStruct((delays * rank, channels), BF16),
            jax.ShapeDtypeStruct((delays * rank, channels), BF16),
        ],
        in_specs=[pl.BlockSpec(memory_space=pltpu.HBM)] * 2,
        out_specs=whole(6),
        scratch_shapes=[
            pltpu.VMEM(omega.shape, F32),
            pltpu.VMEM((rank, margin + block), F32),
            pltpu.SemaphoreType.DMA((steps,)),
            pltpu.SemaphoreType.DMA((delays,)),
        ],
        compiler_params=pltpu.CompilerParams(vmem_limit_bytes=20 * MIB),
        cost_estimate=pl.CostEstimate(flops=4 * WEIGHT, bytes_accessed=samples.size * 4, transcendentals=0),
    )(samples, pltpu.with_memory_space_constraint(omega, pltpu.HBM))


def sketch_middle(middle, samples, high, low, delays):
    rank, inner = middle.shape
    block = samples.shape[1]
    reach = delays - 1
    half = rank // 2

    def body(middle_ref, s_ref, high_ref, low_ref, keep_ref, send_ref, acc_ref):
        acc_ref[...] = middle_ref[...]
        for step in range(reach, block // LAG - reach):
            s_high, s_low = split(s_ref[:, step * LAG : (step + 1) * LAG])
            term = dot3(high_ref[...], low_ref[...], s_high, s_low, NN)
            for d in range(delays):
                acc_ref[:, (step - d) * LAG : (step - d + 1) * LAG] += term[d * rank : (d + 1) * rank, :]
        core = lax.axis_index("core")
        for which, ref in ((core, keep_ref), (1 - core, send_ref)):
            ref[...] = acc_ref[rows_at(which, half), :]

    return call(
        body, [(half, inner)] * 2, [middle, samples, high, low], 16, [(rank, inner)], weight=2 * WEIGHT
    )


def quarters():
    core = lax.axis_index("core")
    own, other = side("y", 0), side("y", 0, 1 - core)
    return [2 * core + own, 2 * (1 - core) + other, 2 * core + 1 - own, 2 * (1 - core) + 1 - other]


def in_order(places):
    return jnp.minimum(*places), jnp.maximum(*places)


def projection_partial(samples, sketch, delays):
    channels, block = samples.shape
    quarter, width = sketch[0].shape
    count = 2 * quarter
    steps = block // WIDE
    lanes = delays * count

    def body(s_ref, mine_ref, other_ref, keep_ref, send_ref, high_ref, low_ref, acc_ref):
        core = lax.axis_index("core")
        for place, ref in ((core, mine_ref), (1 - core, other_ref)):
            high, low = split(ref[...])
            high_ref[rows_at(place, quarter), :] = high
            low_ref[rows_at(place, quarter), :] = low
        acc_ref[...] = jnp.zeros_like(acc_ref)

        @pl.loop(0, steps)
        def _(step):
            s_high, s_low = split(s_ref[:, pl.ds(pl.multiple_of(step * WIDE, WIDE), WIDE)])
            highs, lows = [], []
            for d in range(delays):
                at = pl.ds(pl.multiple_of(step * WIDE + (delays - 1 - d) * LAG, LAG), WIDE)
                highs.append(high_ref[:, at])
                lows.append(low_ref[:, at])
            acc_ref[...] += dot3(s_high, s_low, jnp.concatenate(highs, 0), jnp.concatenate(lows, 0), NT)

        which = side(*ROUTE[0])
        for place, ref in ((which, keep_ref), (1 - which, send_ref)):
            ref[...] = acc_ref[rows_at(place, channels // 2), :]

    return pl.pallas_call(
        body,
        out_shape=[jax.ShapeDtypeStruct((channels // 2, lanes), F32)] * 2,
        in_specs=whole(3),
        out_specs=whole(2),
        scratch_shapes=[
            pltpu.VMEM((count, width), BF16),
            pltpu.VMEM((count, width), BF16),
            pltpu.VMEM((channels, lanes), F32),
        ],
        compiler_params=pltpu.CompilerParams(vmem_limit_bytes=24 * MIB),
        cost_estimate=pl.CostEstimate(flops=4 * WEIGHT, bytes_accessed=channels * block * 4, transcendentals=0),
    )(samples, *sketch)


def fold_with_gram(keep, came, axis, step, sketches, margin):
    quarter, width = sketches[0][0].shape
    rank = 4 * quarter
    count, lanes = keep.shape[0] // 2, keep.shape[1]
    tail = rank * rank // lanes

    def body(a_ref, b_ref, *refs):
        ins, outs, (sketch_ref, gram_ref) = refs[:4], refs[4:6], refs[6:]
        for place, ref in zip(quarters(), ins):
            sketch_ref[rows_at(place, quarter), :] = ref[:, margin:]
        high, low = split(sketch_ref[...])
        gram_ref[...] = dot3(high, low, high, low, NT)
        which = side(axis, step)
        for place, ref in zip((which, 1 - which), outs):
            at = rows_at(place, count)
            ref[:count, :] = a_ref[at, :] + b_ref[at, :]
            for group in range(lanes // rank):
                ref[count:, group * rank : (group + 1) * rank] = gram_ref[group * tail : (group + 1) * tail, :]

    flat = [half for pair in sketches for half in pair]
    scratch = [(rank, width - margin), (rank, rank)]
    return call(body, [(count + tail, lanes)] * 2, [keep, came, *flat], 16, scratch, weight=WEIGHT)


def fold(keep, came, axis, step):
    count = keep.shape[0] // 2

    def body(a_ref, b_ref, keep_ref, send_ref):
        which = side(axis, step)
        for place, ref in ((which, keep_ref), (1 - which, send_ref)):
            at = rows_at(place, count)
            ref[...] = a_ref[at, :] + b_ref[at, :]

    return call(body, [(count, keep.shape[1])] * 2, [keep, came], 8, weight=WEIGHT)


def add(a, b, tail=0):
    count = a.shape[0] - tail

    def body(a_ref, b_ref, out_ref, *tails):
        out_ref[...] = a_ref[:count, :] + b_ref[:count, :]
        for ref in tails:
            ref[...] = a_ref[count:, :] + b_ref[count:, :]

    return call(body, [(count, a.shape[1])] + [(tail, a.shape[1])] * (tail > 0), [a, b], 8, weight=WEIGHT)


def unfold(mine, came, axis, step):
    count = mine.shape[0]

    def body(a_ref, b_ref, out_ref):
        out_ref[rows_at(side(axis, step), count), :] = a_ref[...]
        out_ref[rows_at(1 - side(axis, step), count), :] = b_ref[...]

    return call(body, [(2 * count, mine.shape[1])], [mine, came], 8, weight=WEIGHT)[0]


ROUTE = (("x", 0), ("z", 0), ("z", 1), ("x", 1), ("z", 0), ("x", 0))


def advanced(at, keep, came, tail):
    if at == 4:
        value = unfold(keep, came, *ROUTE[at])
        return value, value, None
    value, *rest = add(keep, came, tail if at == 3 else 0)
    return value, value, *(rest or [None])


def summed_both(first, second, sketches, margin):
    states = [first, second]
    came = [along(*ROUTE[0], state[1]) for state in states]
    for at in range(5):
        for i in range(2):
            arrived, _ = lax.optimization_barrier((came[i], states[1 - i][1]))
            if at > 0:
                tail = 0 if i else states[i][0].shape[0] - first[0].shape[0] // 2
                *states[i], rest = advanced(at, states[i][0], arrived, tail)
                if rest is not None:
                    gram = add(rest, along(*ROUTE[0], rest))[0]
            elif i == 0:
                states[i] = fold_with_gram(states[i][0], arrived, *ROUTE[1], sketches, margin)
            else:
                states[i] = fold(states[i][0], arrived, *ROUTE[1])
            came[i] = along(*ROUTE[at + 1], states[i][1])
    return (states[0][0], came[0]), (states[1][0], came[1]), gram


def inverse_factor(tail, rank):
    deep, delays = tail.shape[0], tail.shape[1] // rank
    panel = 16

    def body(tail_ref, out_ref, left_ref, right_ref):
        for d in range(delays):
            left_ref[d * deep : (d + 1) * deep, :] = tail_ref[:, d * rank : (d + 1) * rank]
        square = (rank, rank)
        same = lax.broadcasted_iota(jnp.int32, square, 0) == lax.broadcasted_iota(jnp.int32, square, 1)
        right_ref[...] = jnp.where(same, 1.0, 0.0)
        row = lax.broadcasted_iota(jnp.int32, (panel, rank), 0)
        for top in range(0, rank, panel):
            end = top + panel
            left, right = left_ref[top:end, :], right_ref[top:end, :]
            columns = [jnp.broadcast_to(left[:, top + m : top + m + 1], (panel, rank)) for m in range(panel)]
            pivots = jnp.zeros((panel, rank), F32)
            for j in range(panel):
                reciprocal = 1.0 / columns[j][j : j + 1, :]
                pivots = jnp.where(row == j, reciprocal, pivots)
                factor = jnp.where(row > j, columns[j] * reciprocal, 0.0)
                for m in range(j + 1, panel):
                    columns[m] = columns[m] - factor * columns[m][j : j + 1, :]
                left = left - factor * left[j : j + 1, :]
                right = right - factor * right[j : j + 1, :]
            if end < rank:
                factors = (left * pivots).T
                below_left, below_right = left_ref[end:, :], right_ref[end:, :]
                for j in range(panel):
                    factor = factors[end:, j : j + 1]
                    below_left = below_left - factor * left[j : j + 1, :]
                    below_right = below_right - factor * right[j : j + 1, :]
                left_ref[end:, :] = below_left
                right_ref[end:, :] = below_right
            out_ref[top:end, :] = right * lax.sqrt(pivots)

    return pl.pallas_call(
        body,
        out_shape=jax.ShapeDtypeStruct((rank, rank), F32),
        in_specs=whole(1),
        out_specs=whole(1)[0],
        scratch_shapes=[pltpu.VMEM((rank, rank), F32)] * 2,
        compiler_params=pltpu.CompilerParams(vmem_limit_bytes=8 * MIB),
    )(tail)


def shards(samples, omega):
    delays, channels, rank = omega.shape
    block = samples.shape[1]
    margin = (delays - 1) * LAG
    inner = block - margin
    width = margin + block
    half, quarter = rank // 2, rank // 4
    total = block * SIDE * SIDE

    ends, ends_send, middle, samples, high, low = sketch_ends(samples, omega)
    middle, middle_send = sketch_middle(middle, samples, high, low, delays)
    ends, ends_send = fold(ends, lax.ppermute(ends_send, "core", [(0, 1), (1, 0)]), "y", 0)
    middle, middle_send = fold(middle, lax.ppermute(middle_send, "core", [(0, 1), (1, 0)]), "y", 0)
    ends_came = along("y", 0, ends_send)
    middle_came = along("y", 0, middle_send)
    (ends,) = add(ends, ends_came)
    ends_came = along("y", 1, ends)
    (middle,) = add(middle, middle_came)
    middle_came = along("y", 1, middle)

    def even():
        return lax.rem(lax.axis_index("z"), 2) == 0

    def add_ends(a_ref, b_ref, left_ref, right_ref, one_ref, two_ref):
        left_ref[...] = a_ref[:, :margin] + b_ref[:, :margin]
        right_ref[...] = a_ref[:, margin:] + b_ref[:, margin:]
        one_ref[...] = jnp.where(even(), right_ref[...], left_ref[...])
        two_ref[...] = jnp.where(even(), left_ref[...], right_ref[...])

    left, right, one, two = call(add_ends, [(quarter, margin)] * 4, [ends, ends_came], 8)
    one, two = paired(one, 0), paired(two, 1)

    def join(left_ref, right_ref, one_ref, two_ref, middle_ref, middle_came_ref, out_ref):
        inside = lax.axis_index("x") + lax.axis_index("z") > 0
        left_came = jnp.where(even(), two_ref[...], one_ref[...])
        right_came = jnp.where(even(), one_ref[...], two_ref[...])
        out_ref[:, :margin] = jnp.where(inside, left_ref[...] + left_came, 0.0)
        out_ref[:, margin:block] = middle_ref[...] + middle_came_ref[...]
        out_ref[:, block:] = right_ref[...] + right_came

    (mine,) = call(join, [(quarter, width)], [left, right, one, two, middle, middle_came], 8)
    sketches = [(mine, lax.ppermute(mine, "core", [(0, 1), (1, 0)]))]
    mine = along("y", 0, mine)

    first = projection_partial(samples, sketches[0], delays)
    mine, *first = lax.optimization_barrier((mine, *first))
    sketches.append((mine, lax.ppermute(mine, "core", [(0, 1), (1, 0)])))
    second = projection_partial(samples, sketches[1], delays)
    first, second, gram = summed_both(first, second, sketches, margin)
    inverse = inverse_factor(gram, rank)

    def multiplied(turned_ref, part, ref, put):
        pick = [turned_ref[rows_at(q, quarter), :] for q in in_order(quarters()[2 * part : 2 * part + 2])]
        none = [jnp.zeros((half, rank), F32)]
        pick = [split(jnp.concatenate(m, 0)) for m in (pick + none, none + pick)]
        for pair in range(delays // 2):
            a_high, a_low = split(ref[:, pair * rank : (pair + 1) * rank])
            for odd in range(2):
                put(2 * pair + odd, dot3(a_high, a_low, *pick[odd], NN))

    def finish_first(inverse_ref, *refs):
        rows, ins, outs, (mine_ref, sketch_ref, sem, both_ref) = refs[:4], refs[4:7], refs[7:11], refs[11:]
        basis_ref, out_ref, partial_ref, turned_ref = outs
        turned_ref[...] = inverse_ref[...].T
        which = side(*ROUTE[0])

        def put_first(place):
            def put(d, value):
                both_ref[d, rows_at(place, channels // 2), :] = value

            return put

        multiplied(turned_ref, 0, ins[0], put_first(which))
        multiplied(turned_ref, 0, ins[1], put_first(1 - which))

        def copy(d):
            return pltpu.make_async_copy(mine_ref.at[d], out_ref.at[d, rows_at(which, channels // 2), :], sem.at[d])

        def put_second(d, value):
            mine_ref[d] = both_ref[d, rows_at(which, channels // 2), :] + value
            copy(d).start()

        multiplied(turned_ref, 1, ins[2], put_second)
        for d in range(delays):
            partial_ref[d] = both_ref[d, rows_at(1 - which, channels // 2), :]
        core, y = lax.axis_index("core"), lax.axis_index("y")
        columns = block // 8
        at = pl.ds(pl.multiple_of(margin + (y * 2 + core) * columns, columns), columns)
        for place, ref in zip(quarters(), rows):
            sketch_ref[rows_at(place, quarter), :] = ref[:, at]
        high, low = split(inverse_ref[...])
        s_high, s_low = split(sketch_ref[...])
        basis_ref[...] = math.sqrt(total) * dot3(high, low, s_high, s_low, NN)
        for d in range(delays):
            copy(d).wait()

    shape, part_shape = (delays, channels, rank), (delays, channels // 2, rank)
    outs = [jax.ShapeDtypeStruct(s, F32) for s in ((rank, block // 8), shape, part_shape, (rank, rank))]
    basis, projection, partial, turned = pl.pallas_call(
        finish_first,
        out_shape=outs,
        in_specs=whole(8),
        out_specs=whole(1) + [pl.BlockSpec(memory_space=pltpu.HBM)] + whole(2),
        scratch_shapes=[
            pltpu.VMEM(part_shape, F32),
            pltpu.VMEM((rank, block // 8), F32),
            pltpu.SemaphoreType.DMA((delays,)),
            pltpu.VMEM(shape, F32),
        ],
        compiler_params=pltpu.CompilerParams(vmem_limit_bytes=24 * MIB),
    )(inverse, *sketches[0], *sketches[1], *first, second[0])

    def finish_second(turned_ref, partial_ref, came_ref, _, out_ref, mine_ref, sem):
        which = 1 - side(*ROUTE[0])

        def copy(d):
            return pltpu.make_async_copy(mine_ref.at[d], out_ref.at[d, rows_at(which, channels // 2), :], sem.at[d])

        def put(d, value):
            mine_ref[d] = partial_ref[d] + value
            copy(d).start()

        multiplied(turned_ref, 1, came_ref, put)
        for d in range(delays):
            copy(d).wait()

    projection = pl.pallas_call(
        finish_second,
        out_shape=outs[1],
        in_specs=whole(3) + [pl.BlockSpec(memory_space=pltpu.HBM)],
        out_specs=pl.BlockSpec(memory_space=pltpu.HBM),
        scratch_shapes=[pltpu.VMEM(part_shape, F32), pltpu.SemaphoreType.DMA((delays,))],
        input_output_aliases={3: 0},
        compiler_params=pltpu.CompilerParams(vmem_limit_bytes=16 * MIB),
    )(turned, partial, second[1], projection)
    return basis, projection


def solution(mesh):
    fine = Mesh(mesh.devices.reshape(SIDE, SIDE, SIDE, 2), AXES)
    tm, chan = ("x", "z"), ("y", "core")
    return jax.shard_map(
        shards,
        mesh=fine,
        in_specs=(P(chan, tm), P(None, chan, None)),
        out_specs=(P(None, tm + chan), P(None, chan, None)),
        check_vma=False,
    )
```
